1024 devices in a mesh: space: 128 (over y, z), chan: 8 (over x, core).
Axes of the slice: x: 4, y: 4, z: 32, core: 2. Of those that a mesh axis runs over, the one named last changes fastest.
Arguments:
- volume: bfloat16 [256, 128, 8, 128], P('chan', 'space'), may hold values from -6 to 6
- kernel: bfloat16 [3, 3, 3, 256, 256], replicated, may hold values from -0.078125 to 0.078125
- cotangent: bfloat16 [256, 128, 8, 128], P('chan', 'space'), may hold values from -6 to 6
Outputs:
- output: bfloat16 [256, 128, 8, 128], P('chan', 'space')
- input_grad: bfloat16 [256, 128, 8, 128], P('chan', 'space')
- weight_grad: float32 [3, 3, 3, 256, 256], P(None, None, None, 'chan')
The draws below stay inside these ranges and needn't reach their ends.
All inputs are finite; a program needn't handle non-finite values.
Results may differ from the reference program's by a relative error of at most 0.001.
Values may be sent and summed in bfloat16 or wider, within the bound.
No kernel may reach another device: no remote copies, remote signals or barrier semaphores. Data moves between devices by JAX's collectives and lax.ppermute only.
A program may use at most 64 MiB of HBM per device.

```python
import math
import jax
import jax.numpy as jnp
from jax import lax

C = 256
NY = 8
NZ = 128
NX = 128


def level_of(stream_key, shape, split, low, high):
    def one(axis_at, parts):
        draws = jax.random.uniform(jax.random.fold_in(jax.random.fold_in(stream_key, 6), axis_at), (parts,), jnp.float32, low / len(split), high / len(split))
        return jnp.repeat(jnp.exp(draws), shape[axis_at] // parts).reshape((-1,) + (1,) * (len(shape) - axis_at - 1))

    factor_of = one(*split[0])
    for cut in split[1:]:
        factor_of = factor_of * one(*cut)
    return factor_of


def gaussian(own_key, shape, scale, most, shards=(), kind=jnp.bfloat16):
    drawn = scale * jax.random.normal(own_key, shape, jnp.float32)
    if shards:
        drawn = drawn * level_of(own_key, shape, shards, -0.22, 0.18)
    return jnp.clip(drawn, -most, most).astype(kind)


def setup_inputs(seed: int = 0) -> dict:
    arg_keys = jax.random.split(jax.random.key(seed), 4)
    return {
        "volume": gaussian(arg_keys[0], (C, NX, NY, NZ), 1.0, 6.0, ((0, 8), (1, 128))),
        "kernel": gaussian(arg_keys[1], (3, 3, 3, C, C), (27 * C) ** -0.5, 0.078125),
        "cotangent": gaussian(arg_keys[2], (C, NX, NY, NZ), 1.0, 6.0, ((0, 8), (1, 128))),
    }


def padded_grid(field):
    return jnp.pad(field, ((0, 0), (1, 1), (1, 1), (1, 1)))

def window(padded, along_x, along_y, along_z, extent):
    planes, height, breadth = extent
    portion = padded[:, along_x:along_x + planes, along_y:along_y + height, along_z:along_z + breadth]
    return portion.reshape(portion.shape[0], -1)

def reference(volume, kernel, cotangent):
    channels = volume.shape[0]
    extent = volume.shape[1:]
    cell_count = extent[0] * extent[1] * extent[2]
    vol_pad = padded_grid(volume)
    cot_pad = padded_grid(cotangent)
    cot_flat = cotangent.reshape(channels, cell_count)
    forward = jnp.zeros((channels, cell_count), jnp.float32)
    backward = jnp.zeros((channels, cell_count), jnp.float32)
    gradients = []
    for along_x in range(3):
        for along_y in range(3):
            for along_z in range(3):
                tap_weight = kernel[along_x, along_y, along_z]
                shifted = window(vol_pad, along_x, along_y, along_z, extent)
                forward = forward + jnp.dot(tap_weight.T, shifted, preferred_element_type=jnp.float32)
                mirrored = window(cot_pad, 2 - along_x, 2 - along_y, 2 - along_z, extent)
                backward = backward + jnp.dot(tap_weight, mirrored, preferred_element_type=jnp.float32)
                gradients.append(lax.dot_general(shifted, cot_flat, (((1,), (1,)), ((), ())), preferred_element_type=jnp.float32))
    factor = 1.0 / math.sqrt(cell_count)
    weight_grad = jnp.stack(gradients).reshape(3, 3, 3, channels, channels) * factor
    output = forward.astype(jnp.bfloat16).reshape(volume.shape)
    input_grad = backward.astype(jnp.bfloat16).reshape(volume.shape)
    return (output, input_grad, weight_grad)
```

```python
import math

import jax
import jax.numpy as jnp
from jax import lax
from jax.experimental import pallas as pl
from jax.experimental.pallas import tpu as pltpu
from jax.sharding import PartitionSpec as P

TAPS = 27
Y_CHIPS = 4
NEAR = 4


def groups_of(count):
    length = count // Y_CHIPS
    far = length // NEAR
    along_y = [[y * length + z for y in range(Y_CHIPS)] for z in range(length)]
    near_z = [
        [y * length + hop * NEAR + k for k in range(NEAR)]
        for y in range(Y_CHIPS)
        for hop in range(far)
    ]
    far_z = [
        [y * length + hop * NEAR + k for hop in range(far)]
        for y in range(Y_CHIPS)
        for k in range(NEAR)
    ]
    return along_y, near_z, far_z


def exchange(pieces, axis, groups=None):
    return lax.all_to_all(pieces, axis, 0, 0, tiled=True, axis_index_groups=groups)


def reduce_pieces(total, axis, groups):
    count = len(groups[0])
    pieces = total.reshape(count, total.shape[0] // count, total.shape[1])
    return jnp.sum(exchange(pieces, axis, groups), axis=0)


def gather_pieces(piece, axis, groups, count):
    whole = exchange(jnp.broadcast_to(piece[None], (count,) + piece.shape), axis, groups)
    return whole.reshape((count * piece.shape[0],) + piece.shape[1:])


def shift_lanes(value, offset, lanes):
    if offset == 0:
        return value
    at = lax.broadcasted_iota(jnp.int32, value.shape, 1)
    if offset < 0:
        return jnp.where(at == 0, 0.0, pltpu.roll(value, 1, 1))
    return jnp.where(at == lanes - 1, 0.0, pltpu.roll(value, lanes - 1, 1))


def weight_kernel(factor, height, breadth, low, own, high, cot, out, stack):
    count = own.shape[0]
    edge = jnp.zeros((9 * count, breadth), stack.dtype)
    stack[:, :breadth] = edge
    stack[:, (height + 1) * breadth :] = edge
    for a, plane in enumerate((low, own, high)):
        for q in range(height):
            row = plane[:, q * breadth : (q + 1) * breadth].astype(jnp.float32)
            for c in range(3):
                at = (a * 3 + c) * count
                stack[at : at + count, (q + 1) * breadth : (q + 2) * breadth] = shift_lanes(
                    row, c - 1, breadth
                ).astype(stack.dtype)
    cells = height * breadth
    group = 3 * count
    for b in range(3):
        part = lax.dot_general(
            stack[:, b * breadth : b * breadth + cells],
            cot[...],
            (((1,), (1,)), ((), ())),
            preferred_element_type=jnp.float32,
        )
        for a in range(3):
            out[(a * 3 + b) * group : (a * 3 + b + 1) * group, :] = (
                part[a * group : (a + 1) * group] * factor
            )
    rest = out.shape[0] - 9 * group
    out[9 * group :, :] = jnp.zeros((rest, out.shape[1]), out.dtype)


def weight_terms(low, own, high, cot, factor, height, breadth):
    count = own.shape[0]
    channels = cot.shape[0]
    rows = (TAPS + 1) * count

    def body(*refs):
        weight_kernel(factor, height, breadth, *refs)

    return pl.pallas_call(
        body,
        out_shape=jax.ShapeDtypeStruct((rows, channels), jnp.float32),
        in_specs=[pl.BlockSpec(memory_space=pltpu.VMEM)] * 4,
        out_specs=pl.BlockSpec(memory_space=pltpu.VMEM),
        scratch_shapes=[pltpu.VMEM((9 * count, (height + 2) * breadth), jnp.bfloat16)],
        compiler_params=pltpu.CompilerParams(vmem_limit_bytes=32 * 1024 * 1024),
        cost_estimate=pl.CostEstimate(
            flops=2 * rows * channels * height * breadth,
            bytes_accessed=4 * rows * channels,
            transcendentals=0,
        ),
    )(low, own, high, cot)


def conv_kernel(mirror, height, breadth, weights, field, out):
    count = out.shape[1]
    for a in range(3):
        part = lax.dot_general(
            weights[a],
            field[...],
            (((1,), (0,)), ((), ())),
            preferred_element_type=jnp.float32,
        )
        for q in range(height):
            total = None
            for c in range(3):
                column = None
                for b in range(3):
                    source = q + (1 - b if mirror else b - 1)
                    if 0 <= source < height:
                        at = (b * 3 + c) * count
                        term = part[at : at + count, source * breadth : (source + 1) * breadth]
                        column = term if column is None else column + term
                moved = shift_lanes(column, 1 - c if mirror else c - 1, breadth)
                total = moved if total is None else total + moved
            out[a, :, q * breadth : (q + 1) * breadth] = total


def conv_terms(weights, field, mirror, height, breadth):
    count = weights.shape[1] // 9
    channels, cells = field.shape

    def body(*refs):
        conv_kernel(mirror, height, breadth, *refs)

    return pl.pallas_call(
        body,
        out_shape=jax.ShapeDtypeStruct((3, count, cells), jnp.float32),
        in_specs=[pl.BlockSpec(memory_space=pltpu.VMEM)] * 2,
        out_specs=pl.BlockSpec(memory_space=pltpu.VMEM),
        compiler_params=pltpu.CompilerParams(vmem_limit_bytes=32 * 1024 * 1024),
        cost_estimate=pl.CostEstimate(
            flops=2 * weights.size * cells,
            bytes_accessed=2 * weights.size + 12 * count * cells,
            transcendentals=0,
        ),
    )(weights, field)


def local(volume, kernel, cotangent):
    count, planes, height, breadth = volume.shape
    cells = height * breadth
    channels = kernel.shape[3]
    slabs = lax.axis_size("space")
    parts = lax.axis_size("chan")
    member = lax.axis_index("chan")
    factor = 1.0 / math.sqrt(slabs * planes * cells)
    along_y, near_z, far_z = groups_of(slabs)
    up = [(i, i + 1) for i in range(slabs - 1)]
    down = [(i + 1, i) for i in range(slabs - 1)]

    vol = volume.reshape(count, cells)
    cot = cotangent.reshape(count, cells)
    vol_low = lax.ppermute(vol, "space", up)
    vol_high = lax.ppermute(vol, "space", down)
    cot_all = exchange(jnp.broadcast_to(cot[None], (parts, count, cells)), "chan")
    cot_all = cot_all.reshape(channels, cells)

    terms = weight_terms(vol_low, vol, vol_high, cot_all, factor, height, breadth)
    terms = reduce_pieces(terms, "space", along_y)
    terms = reduce_pieces(terms, "space", near_z)
    terms = reduce_pieces(terms, "space", far_z)
    total = gather_pieces(terms, "space", far_z, len(far_z[0]))
    total = gather_pieces(total, "space", near_z, len(near_z[0]))
    total = gather_pieces(total, "space", along_y, len(along_y[0]))
    weight_grad = total[: TAPS * count].reshape(3, 3, 3, count, channels)

    vol_all = lax.all_gather(vol, "chan", axis=0, tiled=True)
    fore = lax.dynamic_slice_in_dim(kernel, member * count, count, 4)
    fore = jnp.swapaxes(fore, 3, 4).reshape(3, 9 * count, channels)
    back = lax.dynamic_slice_in_dim(kernel, member * count, count, 3)
    back = back.reshape(3, 9 * count, channels)
    back_terms = conv_terms(back, cot_all, True, height, breadth)
    fore_terms = conv_terms(fore, vol_all, False, height, breadth)

    def finish(own, from_low, from_high):
        whole = own + lax.ppermute(from_low, "space", up) + lax.ppermute(from_high, "space", down)
        return whole.astype(volume.dtype).reshape(volume.shape)

    input_grad = finish(back_terms[1], back_terms[2], back_terms[0])
    output = finish(fore_terms[1], fore_terms[0], fore_terms[2])
    return (output, input_grad, weight_grad)


def solution(mesh):
    return jax.shard_map(
        local,
        mesh=mesh,
        in_specs=(P("chan", "space", None, None), P(), P("chan", "space", None, None)),
        out_specs=(
            P("chan", "space", None, None),
            P("chan", "space", None, None),
            P(None, None, None, "chan", None),
        ),
        check_vma=False,
    )
```

```python
import math

import jax
import jax.numpy as jnp
from jax import lax
from jax.experimental import pallas as pl
from jax.experimental.pallas import tpu as pltpu
from jax.sharding import PartitionSpec as P

TAPS = 27
Y_CHIPS = 4
NEAR = 4


def groups_of(count):
    length = count // Y_CHIPS
    far = length // NEAR
    along_y = [[y * length + z for y in range(Y_CHIPS)] for z in range(length)]
    near_z = [
        [y * length + hop * NEAR + k for k in range(NEAR)]
        for y in range(Y_CHIPS)
        for hop in range(far)
    ]
    block = [
        [y * length + hop * NEAR + k for y in range(Y_CHIPS) for k in range(NEAR)]
        for hop in range(far)
    ]
    far_z = [
        [y * length + hop * NEAR + k for hop in range(far)]
        for y in range(Y_CHIPS)
        for k in range(NEAR)
    ]
    return along_y, near_z, block, far_z


def exchange(pieces, axis, groups=None):
    return lax.all_to_all(pieces, axis, 0, 0, tiled=True, axis_index_groups=groups)


def whole_of(block, parts):
    copies = jnp.broadcast_to(block[None], (parts,) + block.shape)
    return exchange(copies, "chan").reshape((parts * block.shape[0],) + block.shape[1:])


def shift_lanes(value, offset, lanes):
    if offset == 0:
        return value
    at = lax.broadcasted_iota(jnp.int32, value.shape, 1)
    if offset < 0:
        return jnp.where(at == 0, 0.0, pltpu.roll(value, 1, 1))
    return jnp.where(at == lanes - 1, 0.0, pltpu.roll(value, lanes - 1, 1))


def weight_kernel(factor, height, breadth, low, own, high, cot, out, stack):
    count = own.shape[0]
    edge = jnp.zeros((9 * count, breadth), stack.dtype)
    stack[:, :breadth] = edge
    stack[:, (height + 1) * breadth :] = edge
    for a, plane in enumerate((low, own, high)):
        for q in range(height):
            row = plane[:, q * breadth : (q + 1) * breadth].astype(jnp.float32)
            for c in range(3):
                at = (a * 3 + c) * count
                stack[at : at + count, (q + 1) * breadth : (q + 2) * breadth] = shift_lanes(
                    row, c - 1, breadth
                ).astype(stack.dtype)
    cells = height * breadth
    group = 3 * count
    for b in range(3):
        part = lax.dot_general(
            stack[:, b * breadth : b * breadth + cells],
            cot[...],
            (((1,), (1,)), ((), ())),
            preferred_element_type=jnp.float32,
        )
        for a in range(3):
            out[(a * 3 + b) * group : (a * 3 + b + 1) * group, :] = (
                part[a * group : (a + 1) * group] * factor
            )
    rest = out.shape[0] - 9 * group
    out[9 * group :, :] = jnp.zeros((rest, out.shape[1]), out.dtype)


def weight_terms(low, own, high, cot, factor, height, breadth):
    count = own.shape[0]
    channels = cot.shape[0]
    rows = (TAPS + 1) * count

    def body(*refs):
        weight_kernel(factor, height, breadth, *refs)

    return pl.pallas_call(
        body,
        out_shape=jax.ShapeDtypeStruct((rows, channels), jnp.float32),
        in_specs=[pl.BlockSpec()] * 4,
        out_specs=pl.BlockSpec(),
        scratch_shapes=[pltpu.VMEM((9 * count, (height + 2) * breadth), jnp.bfloat16)],
        compiler_params=pltpu.CompilerParams(vmem_limit_bytes=10 * 1024 * 1024),
        cost_estimate=pl.CostEstimate(
            flops=2 * rows * channels * height * breadth,
            bytes_accessed=4 * rows * channels,
            transcendentals=0,
        ),
    )(low, own, high, cot)


def conv_terms(weights, field, mirror, height, breadth, own, up, down):
    count = weights.shape[1] // 9
    places = (down, own, up) if mirror else (up, own, down)
    for a in range(3):
        part = lax.dot_general(
            weights[a],
            field[...],
            (((1,), (0,)), ((), ())),
            preferred_element_type=jnp.float32,
        )
        for q in range(height):
            total = None
            for c in range(3):
                column = None
                for b in range(3):
                    source = q + (1 - b if mirror else b - 1)
                    if 0 <= source < height:
                        at = (b * 3 + c) * count
                        term = part[at : at + count, source * breadth : (source + 1) * breadth]
                        column = term if column is None else column + term
                moved = shift_lanes(column, 1 - c if mirror else c - 1, breadth)
                total = moved if total is None else total + moved
            places[a][:, q * breadth : (q + 1) * breadth] = total


def plane_terms(fore, vol, back, cot, height, breadth):
    count = fore.shape[1] // 9
    cells = vol.shape[1]

    def body(fore_ref, vol_ref, back_ref, cot_ref, own, up, down):
        halves = [pl.ds(0, count), pl.ds(count, count)]
        conv_terms(
            fore_ref, vol_ref, False, height, breadth, *(r.at[halves[0]] for r in (own, up, down))
        )
        conv_terms(
            back_ref, cot_ref, True, height, breadth, *(r.at[halves[1]] for r in (own, up, down))
        )

    shape = jax.ShapeDtypeStruct((2 * count, cells), jnp.float32)
    return pl.pallas_call(
        body,
        out_shape=(shape, shape, shape),
        in_specs=[pl.BlockSpec()] * 4,
        out_specs=(pl.BlockSpec(),) * 3,
        compiler_params=pltpu.CompilerParams(vmem_limit_bytes=10 * 1024 * 1024),
        cost_estimate=pl.CostEstimate(
            flops=4 * fore.size * cells,
            bytes_accessed=4 * fore.size + 24 * count * cells,
            transcendentals=0,
        ),
    )(fore, vol, back, cot)


def local(volume, kernel, cotangent):
    count, planes, height, breadth = volume.shape
    cells = height * breadth
    channels = kernel.shape[3]
    slabs = lax.axis_size("space")
    parts = lax.axis_size("chan")
    member = lax.axis_index("chan")
    factor = 1.0 / math.sqrt(slabs * planes * cells)
    along_y, near_z, block, far_z = groups_of(slabs)
    up = [(i, i + 1) for i in range(slabs - 1)]
    down = [(i + 1, i) for i in range(slabs - 1)]

    cot = cotangent.reshape(count, cells)
    cot_all = whole_of(cot, parts)
    vol = volume.reshape(count, cells)
    vol_low = lax.ppermute(vol, "space", up)
    vol_high = lax.ppermute(vol, "space", down)
    vol_all = lax.all_gather(vol, "chan", axis=0, tiled=True)

    terms = weight_terms(vol_low, vol, vol_high, cot_all, factor, height, breadth)
    pieces = exchange(terms.reshape(len(block[0]), -1, channels), "space", block)
    total = lax.psum(jnp.sum(pieces, axis=0), "space", axis_index_groups=far_z)
    total = lax.all_gather(total, "space", axis=0, tiled=True, axis_index_groups=near_z)
    total = lax.all_gather(total, "space", axis=0, tiled=True, axis_index_groups=along_y)
    weight_grad = total[: TAPS * count].reshape(3, 3, 3, count, channels)

    fore = lax.dynamic_slice_in_dim(kernel, member * count, count, 4)
    fore = jnp.swapaxes(fore, 3, 4).reshape(3, 9 * count, channels)
    back = lax.dynamic_slice_in_dim(kernel, member * count, count, 3)
    back = back.reshape(3, 9 * count, channels)
    own, upper, lower = plane_terms(fore, vol_all, back, cot_all, height, breadth)
    whole = own + lax.ppermute(upper, "space", up) + lax.ppermute(lower, "space", down)
    whole = whole.astype(volume.dtype).reshape((2,) + volume.shape)
    return (whole[0], whole[1], weight_grad)


def solution(mesh):
    return jax.shard_map(
        local,
        mesh=mesh,
        in_specs=(P("chan", "space", None, None), P(), P("chan", "space", None, None)),
        out_specs=(
            P("chan", "space", None, None),
            P("chan", "space", None, None),
            P(None, None, None, "chan", None),
        ),
        check_vma=False,
    )
```

```python
import math

import jax
import jax.numpy as jnp
from jax import lax
from jax.experimental import pallas as pl
from jax.experimental.pallas import tpu as pltpu
from jax.sharding import PartitionSpec as P

TAPS = 27
Y_CHIPS = 4
NEAR = 4


def groups_of(count):
    length = count // Y_CHIPS
    far = length // NEAR
    along_y = [[y * length + z for y in range(Y_CHIPS)] for z in range(length)]
    near_z = [
        [y * length + hop * NEAR + k for k in range(NEAR)]
        for y in range(Y_CHIPS)
        for hop in range(far)
    ]
    block = [
        [y * length + hop * NEAR + k for y in range(Y_CHIPS) for k in range(NEAR)]
        for hop in range(far)
    ]
    far_z = [
        [y * length + hop * NEAR + k for hop in range(far)]
        for y in range(Y_CHIPS)
        for k in range(NEAR)
    ]
    return along_y, near_z, block, far_z


def exchange(pieces, axis, groups=None):
    return lax.all_to_all(pieces, axis, 0, 0, tiled=True, axis_index_groups=groups)


VMEM = pl.BlockSpec(memory_space=pltpu.VMEM)
HBM = pl.BlockSpec(memory_space=pl.ANY)


def limits(mib=56):
    return pltpu.CompilerParams(vmem_limit_bytes=mib * 1024 * 1024)


TOKEN = jax.ShapeDtypeStruct((8, 128), jnp.float32)


def own_weights(kernel, count):
    channels = kernel.shape[2]
    width = min(channels, 128)
    per = width // count

    def body(kernel_ref, fore, back, token, block, sems):
        token[...] = jnp.zeros(token.shape, token.dtype)
        member = lax.axis_index("chan")
        lanes = pl.ds(pl.multiple_of((member // per) * width, width), width)
        rows = pl.ds(pl.multiple_of(member * count, count), count)
        moves = [
            pltpu.make_async_copy(kernel_ref.at[:, :, lanes], block, sems.at[0]),
            pltpu.make_async_copy(kernel_ref.at[:, rows, :], back, sems.at[1]),
        ]
        for move in moves:
            move.start()
        at = lax.broadcasted_iota(jnp.int32, (count, width), 1)
        row = lax.broadcasted_iota(jnp.int32, (count, width), 0)
        pick = jnp.where(at == row + (member % per) * count, 1.0, 0.0).astype(fore.dtype)
        moves[0].wait()
        for tap in range(TAPS):
            fore[tap] = lax.dot_general(
                pick, block[tap], (((1,), (1,)), ((), ())), preferred_element_type=jnp.float32
            ).astype(fore.dtype)
        moves[1].wait()

    shape = jax.ShapeDtypeStruct((TAPS, count, channels), kernel.dtype)
    return pl.pallas_call(
        body,
        out_shape=(shape, shape, TOKEN),
        in_specs=[HBM],
        out_specs=(VMEM, VMEM, VMEM),
        scratch_shapes=[
            pltpu.VMEM((TAPS, channels, width), kernel.dtype),
            pltpu.SemaphoreType.DMA((2,)),
        ],
        compiler_params=limits(),
    )(kernel)


def spread(block, copies):
    count, height, breadth = block.shape
    cells = height * breadth

    def body(block_ref, out, wide, flat, sems):
        wide[...] = block_ref[...].astype(jnp.float32)
        for q in range(height):
            flat[:, q * breadth : (q + 1) * breadth] = wide[:, q, :].astype(flat.dtype)
        moves = [pltpu.make_async_copy(flat, out.at[k], sems.at[k]) for k in range(copies)]
        for move in moves:
            move.start()
        for move in moves:
            move.wait()

    return pl.pallas_call(
        body,
        out_shape=jax.ShapeDtypeStruct((copies, count, cells), block.dtype),
        in_specs=[VMEM],
        out_specs=HBM,
        scratch_shapes=[
            pltpu.VMEM(block.shape, jnp.float32),
            pltpu.VMEM((count, cells), block.dtype),
            pltpu.SemaphoreType.DMA((copies,)),
        ],
        compiler_params=limits(),
    )(block)


def sum_pieces(pieces, after):
    count, rows, columns = pieces.shape

    def body(pieces_ref, after_ref, out):
        total = pieces_ref[0]
        for k in range(1, count):
            total = total + pieces_ref[k]
        out[...] = total

    return pl.pallas_call(
        body,
        out_shape=jax.ShapeDtypeStruct((rows, columns), pieces.dtype),
        in_specs=[VMEM, VMEM],
        out_specs=VMEM,
        compiler_params=limits(8),
        cost_estimate=pl.CostEstimate(
            flops=pieces.size, bytes_accessed=4 * pieces.size, transcendentals=0
        ),
    )(pieces, after)


def repeated(piece, copies):
    def body(piece_ref, out, sems):
        moves = [pltpu.make_async_copy(piece_ref, out.at[k], sems.at[k]) for k in range(copies)]
        for move in moves:
            move.start()
        for move in moves:
            move.wait()

    return pl.pallas_call(
        body,
        out_shape=jax.ShapeDtypeStruct((copies,) + piece.shape, piece.dtype),
        in_specs=[HBM],
        out_specs=HBM,
        scratch_shapes=[pltpu.SemaphoreType.DMA((copies,))],
        compiler_params=limits(),
    )(piece)


def finish(own, low, high, height, breadth, dtype, after):
    rows = own.shape[0]
    count = rows // 2

    def body(own_ref, low_ref, high_ref, after_ref, first, second, wide):
        for q in range(height):
            lanes = pl.ds(q * breadth, breadth)
            wide[:, q, :] = own_ref[:, lanes] + low_ref[:, lanes] + high_ref[:, lanes]
        first[...] = wide[:count].astype(dtype)
        second[...] = wide[count:].astype(dtype)

    shape = jax.ShapeDtypeStruct((count, height, breadth), dtype)
    return pl.pallas_call(
        body,
        out_shape=(shape, shape),
        in_specs=[VMEM] * 3 + [HBM],
        out_specs=(VMEM, VMEM),
        scratch_shapes=[pltpu.VMEM((rows, height, breadth), jnp.float32)],
        compiler_params=limits(8),
    )(own, low, high, after)


def shift_lanes(value, offset, lanes):
    if offset == 0:
        return value
    at = lax.broadcasted_iota(jnp.int32, value.shape, 1)
    if offset < 0:
        return jnp.where(at == 0, 0.0, pltpu.roll(value, 1, 1))
    return jnp.where(at == lanes - 1, 0.0, pltpu.roll(value, lanes - 1, 1))


def weight_terms(low, own, high, cot, after, factor, height, breadth):
    count, cells = own.shape
    channels = cot.shape[0]
    group = 3 * count
    rows = 9 * group + count

    def body(low_ref, own_ref, high_ref, cot_ref, after_ref, *rest):
        out, planes, field, stack, held, in_sems, out_sems = rest
        sources = (low_ref, own_ref, high_ref)
        moves = [
            pltpu.make_async_copy(source, planes.at[k], in_sems.at[k])
            for k, source in enumerate(sources)
        ]
        moves.append(pltpu.make_async_copy(cot_ref, field, in_sems.at[3]))
        for move in moves:
            move.start()
        sent = []

        def send(start, size):
            move = pltpu.make_async_copy(
                held.at[pl.ds(start, size)], out.at[pl.ds(start, size)], out_sems.at[len(sent)]
            )
            move.start()
            sent.append(move)

        held[9 * group :, :] = jnp.zeros((count, channels), held.dtype)
        send(9 * group, count)
        edge = jnp.zeros((9 * count, breadth), stack.dtype)
        stack[:, :breadth] = edge
        stack[:, (height + 1) * breadth :] = edge
        for a in range(3):
            moves[a].wait()
            for q in range(height):
                row = planes[a, :, q * breadth : (q + 1) * breadth].astype(jnp.float32)
                for c in range(3):
                    at = (a * 3 + c) * count
                    stack[at : at + count, (q + 1) * breadth : (q + 2) * breadth] = shift_lanes(
                        row, c - 1, breadth
                    ).astype(stack.dtype)
        moves[3].wait()
        for b in range(3):
            part = lax.dot_general(
                stack[:, b * breadth : b * breadth + cells],
                field[...],
                (((1,), (1,)), ((), ())),
                preferred_element_type=jnp.float32,
            )
            for a in range(3):
                at = (a * 3 + b) * group
                held[at : at + group, :] = part[a * group : (a + 1) * group] * factor
                send(at, group)
        for move in sent:
            move.wait()

    return pl.pallas_call(
        body,
        out_shape=jax.ShapeDtypeStruct((rows, channels), jnp.float32),
        in_specs=[HBM] * 5,
        out_specs=HBM,
        scratch_shapes=[
            pltpu.VMEM((3, count, cells), own.dtype),
            pltpu.VMEM((channels, cells), cot.dtype),
            pltpu.VMEM((9 * count, cells + 2 * breadth), own.dtype),
            pltpu.VMEM((rows, channels), jnp.float32),
            pltpu.SemaphoreType.DMA((4,)),
            pltpu.SemaphoreType.DMA((10,)),
        ],
        compiler_params=limits(),
        cost_estimate=pl.CostEstimate(
            flops=2 * rows * channels * cells,
            bytes_accessed=4 * rows * channels,
            transcendentals=0,
        ),
    )(low, own, high, cot, after)


def conv_terms(weights, field, mirror, height, breadth, own, up, down):
    count = weights.shape[1] // 9
    places = (down, own, up) if mirror else (up, own, down)
    for a in range(3):
        part = lax.dot_general(
            weights[a],
            field[...],
            (((1,), (0,)), ((), ())),
            preferred_element_type=jnp.float32,
        )
        for q in range(height):
            total = None
            for c in range(3):
                column = None
                for b in range(3):
                    source = q + (1 - b if mirror else b - 1)
                    if 0 <= source < height:
                        at = (b * 3 + c) * count
                        term = part[at : at + count, source * breadth : (source + 1) * breadth]
                        column = term if column is None else column + term
                moved = shift_lanes(column, 1 - c if mirror else c - 1, breadth)
                total = moved if total is None else total + moved
            places[a][:, q * breadth : (q + 1) * breadth] = total


def plane_terms(fore, vol, back, cot, height, breadth):
    count = fore.shape[1] // 9
    cells = vol.shape[1]

    def body(fore_ref, vol_ref, back_ref, cot_ref, own, up, down, token):
        token[...] = jnp.zeros(token.shape, token.dtype)
        halves = [pl.ds(0, count), pl.ds(count, count)]
        conv_terms(
            fore_ref, vol_ref, False, height, breadth, *(r.at[halves[0]] for r in (own, up, down))
        )
        conv_terms(
            back_ref, cot_ref, True, height, breadth, *(r.at[halves[1]] for r in (own, up, down))
        )

    shape = jax.ShapeDtypeStruct((2 * count, cells), jnp.float32)
    return pl.pallas_call(
        body,
        out_shape=(shape, shape, shape, TOKEN),
        in_specs=[VMEM] * 4,
        out_specs=(VMEM,) * 4,
        compiler_params=limits(12),
        cost_estimate=pl.CostEstimate(
            flops=4 * fore.size * cells,
            bytes_accessed=4 * fore.size + 24 * count * cells,
            transcendentals=0,
        ),
    )(fore, vol, back, cot)


def local(volume, kernel, cotangent):
    count, planes, height, breadth = volume.shape
    cells = height * breadth
    channels = kernel.shape[3]
    slabs = lax.axis_size("space")
    parts = lax.axis_size("chan")
    member = lax.axis_index("chan")
    factor = 1.0 / math.sqrt(slabs * planes * cells)
    along_y, near_z, block, far_z = groups_of(slabs)
    up = [(i, i + 1) for i in range(slabs - 1)]
    down = [(i + 1, i) for i in range(slabs - 1)]

    cot_copies = spread(cotangent.reshape(count, height, breadth), parts)
    cot_all = exchange(cot_copies, "chan").reshape(channels, cells)
    vol = volume.reshape(count, cells)
    vol_low = lax.ppermute(vol, "space", up)
    vol_high = lax.ppermute(vol, "space", down)
    fore, back, ready = own_weights(kernel.reshape(TAPS, channels, channels), count)
    fore = fore.reshape(3, 9 * count, channels)
    back = back.reshape(3, 9 * count, channels)

    terms = weight_terms(vol_low, vol, vol_high, cot_all, ready, factor, height, breadth)
    pieces = exchange(terms.reshape(len(block[0]), -1, channels), "space", block)
    vol_all = lax.all_gather(vol, "chan", axis=0, tiled=True)
    own, upper, lower, done = plane_terms(fore, vol_all, back, cot_all, height, breadth)
    total = lax.psum(sum_pieces(pieces, done), "space", axis_index_groups=far_z)
    near = exchange(repeated(total, len(near_z[0])), "space", near_z).reshape(-1, channels)
    whole = exchange(repeated(near, len(along_y[0])), "space", along_y).reshape(-1, channels)
    weight_grad = whole[: TAPS * count].reshape(3, 3, 3, count, channels)

    from_low = lax.ppermute(upper, "space", up)
    from_high = lax.ppermute(lower, "space", down)
    output, input_grad = finish(own, from_low, from_high, height, breadth, volume.dtype, near)
    return (output.reshape(volume.shape), input_grad.reshape(volume.shape), weight_grad)


def solution(mesh):
    return jax.shard_map(
        local,
        mesh=mesh,
        in_specs=(P("chan", "space", None, None), P(), P("chan", "space", None, None)),
        out_specs=(
            P("chan", "space", None, None),
            P("chan", "space", None, None),
            P(None, None, None, "chan", None),
        ),
        check_vma=False,
    )
```

```python
import math

import jax
import jax.numpy as jnp
from jax import lax
from jax.experimental import pallas as pl
from jax.experimental.pallas import tpu as pltpu
from jax.sharding import PartitionSpec as P

TAPS = 27
Y_CHIPS = 4
NEAR = 4


def groups_of(count):
    length = count // Y_CHIPS
    far = length // NEAR
    block = [
        [y * length + hop * NEAR + k for y in range(Y_CHIPS) for k in range(NEAR)]
        for hop in range(far)
    ]
    far_z = [
        [y * length + hop * NEAR + k for hop in range(far)]
        for y in range(Y_CHIPS)
        for k in range(NEAR)
    ]
    return block, far_z


def exchange(pieces, axis, groups=None):
    return lax.all_to_all(pieces, axis, 0, 0, tiled=True, axis_index_groups=groups)


VMEM = pl.BlockSpec(memory_space=pltpu.VMEM)
HBM = pl.BlockSpec(memory_space=pl.ANY)


def limits(mib=56):
    return pltpu.CompilerParams(vmem_limit_bytes=mib * 1024 * 1024)


TOKEN = jax.ShapeDtypeStruct((8, 128), jnp.float32)


def own_weights(kernel, count):
    channels = kernel.shape[2]
    width = min(channels, 128)
    per = width // count

    def body(kernel_ref, fore, back, token, block, sems):
        token[...] = jnp.zeros(token.shape, token.dtype)
        member = lax.axis_index("chan")
        lanes = pl.ds(pl.multiple_of((member // per) * width, width), width)
        rows = pl.ds(pl.multiple_of(member * count, count), count)
        moves = [
            pltpu.make_async_copy(kernel_ref.at[:, :, lanes], block, sems.at[0]),
            pltpu.make_async_copy(kernel_ref.at[:, rows, :], back, sems.at[1]),
        ]
        for move in moves:
            move.start()
        at = lax.broadcasted_iota(jnp.int32, (count, width), 1)
        row = lax.broadcasted_iota(jnp.int32, (count, width), 0)
        pick = jnp.where(at == row + (member % per) * count, 1.0, 0.0).astype(fore.dtype)
        moves[0].wait()
        for tap in range(TAPS):
            fore[tap] = lax.dot_general(
                pick, block[tap], (((1,), (1,)), ((), ())), preferred_element_type=jnp.float32
            ).astype(fore.dtype)
        moves[1].wait()

    shape = jax.ShapeDtypeStruct((TAPS, count, channels), kernel.dtype)
    return pl.pallas_call(
        body,
        out_shape=(shape, shape, TOKEN),
        in_specs=[HBM],
        out_specs=(VMEM, VMEM, VMEM),
        scratch_shapes=[
            pltpu.VMEM((TAPS, channels, width), kernel.dtype),
            pltpu.SemaphoreType.DMA((2,)),
        ],
        compiler_params=limits(),
    )(kernel)


def spread(block, copies):
    count, height, breadth = block.shape
    cells = height * breadth

    def body(block_ref, out, wide, flat, sems):
        wide[...] = block_ref[...].astype(jnp.float32)
        for q in range(height):
            flat[:, q * breadth : (q + 1) * breadth] = wide[:, q, :].astype(flat.dtype)
        moves = [pltpu.make_async_copy(flat, out.at[k], sems.at[k]) for k in range(copies)]
        for move in moves:
            move.start()
        for move in moves:
            move.wait()

    return pl.pallas_call(
        body,
        out_shape=jax.ShapeDtypeStruct((copies, count, cells), block.dtype),
        in_specs=[VMEM],
        out_specs=HBM,
        scratch_shapes=[
            pltpu.VMEM(block.shape, jnp.float32),
            pltpu.VMEM((count, cells), block.dtype),
            pltpu.SemaphoreType.DMA((copies,)),
        ],
        compiler_params=limits(),
    )(block)


def sum_pieces(pieces, after):
    count, rows, columns = pieces.shape

    def body(pieces_ref, after_ref, out):
        total = pieces_ref[0]
        for k in range(1, count):
            total = total + pieces_ref[k]
        out[...] = total

    return pl.pallas_call(
        body,
        out_shape=jax.ShapeDtypeStruct((rows, columns), pieces.dtype),
        in_specs=[VMEM, VMEM],
        out_specs=VMEM,
        compiler_params=limits(8),
        cost_estimate=pl.CostEstimate(
            flops=pieces.size, bytes_accessed=4 * pieces.size, transcendentals=0
        ),
    )(pieces, after)


def repeated(piece, copies):
    def body(piece_ref, out, sems):
        moves = [pltpu.make_async_copy(piece_ref, out.at[k], sems.at[k]) for k in range(copies)]
        for move in moves:
            move.start()
        for move in moves:
            move.wait()

    return pl.pallas_call(
        body,
        out_shape=jax.ShapeDtypeStruct((copies,) + piece.shape, piece.dtype),
        in_specs=[VMEM],
        out_specs=HBM,
        scratch_shapes=[pltpu.SemaphoreType.DMA((copies,))],
        compiler_params=limits(),
    )(piece)


def finish(own, low, high, height, breadth, dtype, after):
    rows = own.shape[0]
    count = rows // 2

    def body(own_ref, low_ref, high_ref, after_ref, first, second, wide):
        for q in range(height):
            lanes = pl.ds(q * breadth, breadth)
            wide[:, q, :] = own_ref[:, lanes] + low_ref[:, lanes] + high_ref[:, lanes]
        first[...] = wide[:count].astype(dtype)
        second[...] = wide[count:].astype(dtype)

    shape = jax.ShapeDtypeStruct((count, height, breadth), dtype)
    return pl.pallas_call(
        body,
        out_shape=(shape, shape),
        in_specs=[VMEM] * 3 + [HBM],
        out_specs=(VMEM, VMEM),
        scratch_shapes=[pltpu.VMEM((rows, height, breadth), jnp.float32)],
        compiler_params=limits(8),
    )(own, low, high, after)


def shift_lanes(value, offset, lanes):
    if offset == 0:
        return value
    at = lax.broadcasted_iota(jnp.int32, value.shape, 1)
    if offset < 0:
        return jnp.where(at == 0, 0.0, pltpu.roll(value, 1, 1))
    return jnp.where(at == lanes - 1, 0.0, pltpu.roll(value, lanes - 1, 1))


def weight_terms(low, own, high, cot, after, factor, height, breadth):
    count, cells = own.shape
    channels = cot.shape[0]
    group = 3 * count
    rows = 9 * group + count

    def body(low_ref, own_ref, high_ref, cot_ref, after_ref, *rest):
        out, planes, field, stack, held, in_sems, out_sems = rest
        sources = (low_ref, own_ref, high_ref)
        moves = [
            pltpu.make_async_copy(source, planes.at[k], in_sems.at[k])
            for k, source in enumerate(sources)
        ]
        moves.append(pltpu.make_async_copy(cot_ref, field, in_sems.at[3]))
        for move in moves:
            move.start()
        sent = []

        def send(start, size):
            move = pltpu.make_async_copy(
                held.at[pl.ds(start, size)], out.at[pl.ds(start, size)], out_sems.at[len(sent)]
            )
            move.start()
            sent.append(move)

        held[9 * group :, :] = jnp.zeros((count, channels), held.dtype)
        send(9 * group, count)
        edge = jnp.zeros((9 * count, breadth), stack.dtype)
        stack[:, :breadth] = edge
        stack[:, (height + 1) * breadth :] = edge
        for a in range(3):
            moves[a].wait()
            for q in range(height):
                row = planes[a, :, q * breadth : (q + 1) * breadth].astype(jnp.float32)
                for c in range(3):
                    at = (a * 3 + c) * count
                    stack[at : at + count, (q + 1) * breadth : (q + 2) * breadth] = shift_lanes(
                        row, c - 1, breadth
                    ).astype(stack.dtype)
        moves[3].wait()
        for b in range(3):
            part = lax.dot_general(
                stack[:, b * breadth : b * breadth + cells],
                field[...],
                (((1,), (1,)), ((), ())),
                preferred_element_type=jnp.float32,
            )
            for a in range(3):
                at = (a * 3 + b) * group
                held[at : at + group, :] = part[a * group : (a + 1) * group] * factor
                send(at, group)
        for move in sent:
            move.wait()

    return pl.pallas_call(
        body,
        out_shape=jax.ShapeDtypeStruct((rows, channels), jnp.float32),
        in_specs=[HBM] * 5,
        out_specs=HBM,
        scratch_shapes=[
            pltpu.VMEM((3, count, cells), own.dtype),
            pltpu.VMEM((channels, cells), cot.dtype),
            pltpu.VMEM((9 * count, cells + 2 * breadth), own.dtype),
            pltpu.VMEM((rows, channels), jnp.float32),
            pltpu.SemaphoreType.DMA((4,)),
            pltpu.SemaphoreType.DMA((10,)),
        ],
        compiler_params=limits(),
        cost_estimate=pl.CostEstimate(
            flops=2 * rows * channels * cells,
            bytes_accessed=4 * rows * channels,
            transcendentals=0,
        ),
    )(low, own, high, cot, after)


def conv_terms(weights, field, mirror, height, breadth, own, up, down):
    count = weights.shape[1] // 9
    places = (down, own, up) if mirror else (up, own, down)
    for a in range(3):
        part = lax.dot_general(
            weights[a],
            field[...],
            (((1,), (0,)), ((), ())),
            preferred_element_type=jnp.float32,
        )
        for q in range(height):
            total = None
            for c in range(3):
                column = None
                for b in range(3):
                    source = q + (1 - b if mirror else b - 1)
                    if 0 <= source < height:
                        at = (b * 3 + c) * count
                        term = part[at : at + count, source * breadth : (source + 1) * breadth]
                        column = term if column is None else column + term
                moved = shift_lanes(column, 1 - c if mirror else c - 1, breadth)
                total = moved if total is None else total + moved
            places[a][:, q * breadth : (q + 1) * breadth] = total


def plane_terms(fore, vol, back, cot, height, breadth):
    count = fore.shape[1] // 9
    cells = vol.shape[1]

    def body(fore_ref, vol_ref, back_ref, cot_ref, own, up, down, token):
        token[...] = jnp.zeros(token.shape, token.dtype)
        halves = [pl.ds(0, count), pl.ds(count, count)]
        conv_terms(
            fore_ref, vol_ref, False, height, breadth, *(r.at[halves[0]] for r in (own, up, down))
        )
        conv_terms(
            back_ref, cot_ref, True, height, breadth, *(r.at[halves[1]] for r in (own, up, down))
        )

    shape = jax.ShapeDtypeStruct((2 * count, cells), jnp.float32)
    return pl.pallas_call(
        body,
        out_shape=(shape, shape, shape, TOKEN),
        in_specs=[VMEM] * 4,
        out_specs=(VMEM,) * 4,
        compiler_params=limits(12),
        cost_estimate=pl.CostEstimate(
            flops=4 * fore.size * cells,
            bytes_accessed=4 * fore.size + 24 * count * cells,
            transcendentals=0,
        ),
    )(fore, vol, back, cot)


def local(volume, kernel, cotangent):
    count, planes, height, breadth = volume.shape
    cells = height * breadth
    channels = kernel.shape[3]
    slabs = lax.axis_size("space")
    parts = lax.axis_size("chan")
    member = lax.axis_index("chan")
    factor = 1.0 / math.sqrt(slabs * planes * cells)
    block, far_z = groups_of(slabs)
    up = [(i, i + 1) for i in range(slabs - 1)]
    down = [(i + 1, i) for i in range(slabs - 1)]

    cot_copies = spread(cotangent.reshape(count, height, breadth), parts)
    cot_all = exchange(cot_copies, "chan").reshape(channels, cells)
    vol = volume.reshape(count, cells)
    vol_low = lax.ppermute(vol, "space", up)
    vol_high = lax.ppermute(vol, "space", down)
    fore, back, ready = own_weights(kernel.reshape(TAPS, channels, channels), count)
    fore = fore.reshape(3, 9 * count, channels)
    back = back.reshape(3, 9 * count, channels)

    terms = weight_terms(vol_low, vol, vol_high, cot_all, ready, factor, height, breadth)
    pieces = exchange(terms.reshape(len(block[0]), -1, channels), "space", block)
    vol_all = lax.all_gather(vol, "chan", axis=0, tiled=True)
    own, upper, lower, done = plane_terms(fore, vol_all, back, cot_all, height, breadth)
    total = lax.psum(sum_pieces(pieces, done), "space", axis_index_groups=far_z)
    whole = exchange(repeated(total, len(block[0])), "space", block).reshape(-1, channels)
    weight_grad = whole[: TAPS * count].reshape(3, 3, 3, count, channels)

    from_low = lax.ppermute(upper, "space", up)
    from_high = lax.ppermute(lower, "space", down)
    output, input_grad = finish(own, from_low, from_high, height, breadth, volume.dtype, total)
    return (output.reshape(volume.shape), input_grad.reshape(volume.shape), weight_grad)


def solution(mesh):
    return jax.shard_map(
        local,
        mesh=mesh,
        in_specs=(P("chan", "space", None, None), P(), P("chan", "space", None, None)),
        out_specs=(
            P("chan", "space", None, None),
            P("chan", "space", None, None),
            P(None, None, None, "chan", None),
        ),
        check_vma=False,
    )
```

```python
import math

import jax
import jax.numpy as jnp
from jax import lax
from jax.experimental import pallas as pl
from jax.experimental.pallas import tpu as pltpu
from jax.sharding import PartitionSpec as P

TAPS = 27
Y_CHIPS = 4
NEAR = 4


def groups_of(count):
    length = count // Y_CHIPS
    far = length // NEAR
    along_y = [[y * length + z for y in range(Y_CHIPS)] for z in range(length)]
    near_z = [[hop * NEAR + k for k in range(NEAR)] for hop in range(count // NEAR)]
    block = [
        [y * length + hop * NEAR + k for y in range(Y_CHIPS) for k in range(NEAR)]
        for hop in range(far)
    ]
    far_z = [
        [y * length + hop * NEAR + k for hop in range(far)]
        for y in range(Y_CHIPS)
        for k in range(NEAR)
    ]
    return along_y, near_z, block, far_z


def exchange(pieces, axis, groups=None):
    return lax.all_to_all(pieces, axis, 0, 0, tiled=True, axis_index_groups=groups)


VMEM = pl.BlockSpec(memory_space=pltpu.VMEM)
HBM = pl.BlockSpec(memory_space=pl.ANY)


def limits(mib=56):
    return pltpu.CompilerParams(vmem_limit_bytes=mib * 1024 * 1024)


TOKEN = jax.ShapeDtypeStruct((8, 128), jnp.float32)


def own_weights(kernel, count):
    channels = kernel.shape[2]
    width = min(channels, 128)
    per = width // count

    def body(kernel_ref, fore, back, token, block, sems):
        token[...] = jnp.zeros(token.shape, token.dtype)
        member = lax.axis_index("chan")
        lanes = pl.ds(pl.multiple_of((member // per) * width, width), width)
        rows = pl.ds(pl.multiple_of(member * count, count), count)
        moves = [
            pltpu.make_async_copy(kernel_ref.at[:, :, lanes], block, sems.at[0]),
            pltpu.make_async_copy(kernel_ref.at[:, rows, :], back, sems.at[1]),
        ]
        for move in moves:
            move.start()
        at = lax.broadcasted_iota(jnp.int32, (count, width), 1)
        row = lax.broadcasted_iota(jnp.int32, (count, width), 0)
        pick = jnp.where(at == row + (member % per) * count, 1.0, 0.0).astype(fore.dtype)
        moves[0].wait()
        for tap in range(TAPS):
            fore[tap] = lax.dot_general(
                pick, block[tap], (((1,), (1,)), ((), ())), preferred_element_type=jnp.float32
            ).astype(fore.dtype)
        moves[1].wait()

    shape = jax.ShapeDtypeStruct((TAPS, count, channels), kernel.dtype)
    return pl.pallas_call(
        body,
        out_shape=(shape, shape, TOKEN),
        in_specs=[HBM],
        out_specs=(VMEM, VMEM, VMEM),
        scratch_shapes=[
            pltpu.VMEM((TAPS, channels, width), kernel.dtype),
            pltpu.SemaphoreType.DMA((2,)),
        ],
        compiler_params=limits(),
    )(kernel)


def flat(block, after):
    count, height, breadth = block.shape

    def body(block_ref, after_ref, out, wide, narrow, sem):
        wide[...] = block_ref[...].astype(jnp.float32)
        for q in range(height):
            narrow[:, q * breadth : (q + 1) * breadth] = wide[:, q, :].astype(narrow.dtype)
        move = pltpu.make_async_copy(narrow, out, sem)
        move.start()
        move.wait()

    shape = (count, height * breadth)
    return pl.pallas_call(
        body,
        out_shape=jax.ShapeDtypeStruct(shape, block.dtype),
        in_specs=[VMEM, HBM],
        out_specs=HBM,
        scratch_shapes=[
            pltpu.VMEM(block.shape, jnp.float32),
            pltpu.VMEM(shape, block.dtype),
            pltpu.SemaphoreType.DMA,
        ],
        compiler_params=limits(),
    )(block, after)


def stacked(first, second, copies, after):
    count, cells = first.shape

    def body(first_ref, second_ref, after_ref, out, sems):
        moves = []
        for k in range(copies):
            for half, source in enumerate((first_ref, second_ref)):
                rows = pl.ds(half * count, count)
                moves.append(
                    pltpu.make_async_copy(source, out.at[k, rows], sems.at[2 * k + half])
                )
        for move in moves:
            move.start()
        for move in moves:
            move.wait()

    return pl.pallas_call(
        body,
        out_shape=jax.ShapeDtypeStruct((copies, 2 * count, cells), first.dtype),
        in_specs=[VMEM, VMEM, HBM],
        out_specs=HBM,
        scratch_shapes=[pltpu.SemaphoreType.DMA((2 * copies,))],
        compiler_params=limits(),
    )(first, second, after)


def sum_pieces(pieces, after):
    count, rows, columns = pieces.shape

    def body(pieces_ref, after_ref, out):
        total = pieces_ref[0]
        for k in range(1, count):
            total = total + pieces_ref[k]
        out[...] = total

    return pl.pallas_call(
        body,
        out_shape=jax.ShapeDtypeStruct((rows, columns), pieces.dtype),
        in_specs=[VMEM, VMEM],
        out_specs=VMEM,
        compiler_params=limits(8),
        cost_estimate=pl.CostEstimate(
            flops=pieces.size, bytes_accessed=4 * pieces.size, transcendentals=0
        ),
    )(pieces, after)


def repeated(piece, copies, after):
    def body(piece_ref, after_ref, out, sems):
        moves = [pltpu.make_async_copy(piece_ref, out.at[k], sems.at[k]) for k in range(copies)]
        for move in moves:
            move.start()
        for move in moves:
            move.wait()

    return pl.pallas_call(
        body,
        out_shape=jax.ShapeDtypeStruct((copies,) + piece.shape, piece.dtype),
        in_specs=[VMEM, HBM],
        out_specs=HBM,
        scratch_shapes=[pltpu.SemaphoreType.DMA((copies,))],
        compiler_params=limits(),
    )(piece, after)


def finish(own, low, high, height, breadth, dtype, after):
    rows = own.shape[0]
    count = rows // 2

    def body(own_ref, low_ref, high_ref, after_ref, first, second, wide):
        for q in range(height):
            lanes = pl.ds(q * breadth, breadth)
            wide[:, q, :] = own_ref[:, lanes] + low_ref[:, lanes] + high_ref[:, lanes]
        first[...] = wide[:count].astype(dtype)
        second[...] = wide[count:].astype(dtype)

    shape = jax.ShapeDtypeStruct((count, height, breadth), dtype)
    return pl.pallas_call(
        body,
        out_shape=(shape, shape),
        in_specs=[VMEM] * 3 + [HBM],
        out_specs=(VMEM, VMEM),
        scratch_shapes=[pltpu.VMEM((rows, height, breadth), jnp.float32)],
        compiler_params=limits(8),
    )(own, low, high, after)


def shift_lanes(value, offset, lanes):
    if offset == 0:
        return value
    at = lax.broadcasted_iota(jnp.int32, value.shape, 1)
    if offset < 0:
        return jnp.where(at == 0, 0.0, pltpu.roll(value, 1, 1))
    return jnp.where(at == lanes - 1, 0.0, pltpu.roll(value, lanes - 1, 1))


def weight_terms(planes, field, vol, cot, factor, height, breadth):
    run, double, cells = planes.shape
    count = double // 2
    share = count // run
    parts = field.shape[0] // count
    outs = parts * share
    group = 9 * count
    wide = -(-group // 128) * 128
    columns = -(-3 * group // 128) * 128

    def body(planes_ref, field_ref, vol_ref, cot_ref, out, both, stack, spots, held, sems):
        moves = [
            pltpu.make_async_copy(vol_ref, both.at[pl.ds(0, count)], sems.at[0]),
            pltpu.make_async_copy(cot_ref, both.at[pl.ds(count, count)], sems.at[1]),
            pltpu.make_async_copy(held, out, sems.at[2]),
        ]
        moves[0].start()
        moves[1].start()
        sources = [(0, count)] + [(k, 0) for k in range(run)] + [(run - 1, count)]
        for m, (k, start) in enumerate(sources):
            for q in range(height):
                lanes = slice(q * breadth, (q + 1) * breadth)
                row = planes_ref[k, start : start + count, lanes].astype(jnp.float32)
                for c in range(3):
                    at = (m * 3 + c) * count
                    stack[at : at + count, lanes] = shift_lanes(row, c - 1, breadth).astype(
                        stack.dtype
                    )
        used = 3 * (run + 2) * count
        stack[used:, :] = jnp.zeros((stack.shape[0] - used, cells), stack.dtype)

        for part in range(parts):
            rows = field_ref[part * count : (part + 1) * count, :].astype(jnp.float32)
            for p in range(run):
                own = rows[p * share : (p + 1) * share, :]
                at = part * share
                spots[p, outs + at : outs + at + share, :] = own
                spots[p, at : at + share, : cells - breadth] = own[:, breadth:]
                spots[p, 2 * outs + at : 2 * outs + at + share, breadth:] = own[:, : cells - breadth]
        for p in range(run):
            edge = jnp.zeros((outs, breadth), spots.dtype)
            spots[p, :outs, cells - breadth :] = edge
            spots[p, 2 * outs :, :breadth] = edge

        total = None
        for p in range(run):
            part = lax.dot_general(
                spots[p].astype(stack.dtype),
                stack[3 * p * count : 3 * p * count + wide, :],
                (((1,), (1,)), ((), ())),
                preferred_element_type=jnp.float32,
            )
            total = part if total is None else total + part
        at = lax.broadcasted_iota(jnp.int32, total.shape, 1)
        total = jnp.where(at < group, total * factor, 0.0)
        held[...] = jnp.zeros(held.shape, held.dtype)
        for b in range(3):
            start = b * group // 128 * 128
            shift = b * group - start
            rows = total[b * outs : (b + 1) * outs, :]
            if shift:
                rows = pltpu.roll(rows, shift, 1)
            held[:, start : start + wide] = held[:, start : start + wide] + rows
        moves[2].start()
        for move in moves:
            move.wait()

    return pl.pallas_call(
        body,
        out_shape=(
            jax.ShapeDtypeStruct((outs, columns), jnp.float32),
            jax.ShapeDtypeStruct((double, cells), planes.dtype),
        ),
        in_specs=[VMEM] * 4,
        out_specs=(HBM, HBM),
        scratch_shapes=[
            pltpu.VMEM((3 * (run - 1) * count + wide, cells), planes.dtype),
            pltpu.VMEM((run, 3 * outs, cells), jnp.float32),
            pltpu.VMEM((outs, columns), jnp.float32),
            pltpu.SemaphoreType.DMA((3,)),
        ],
        compiler_params=limits(32),
        cost_estimate=pl.CostEstimate(
            flops=2 * run * 3 * outs * wide * cells,
            bytes_accessed=4 * outs * columns,
            transcendentals=0,
        ),
    )(planes, field, vol, cot)


def in_order(pieces, count, parts):
    amount, rows, columns = pieces.shape
    run = amount // Y_CHIPS
    share = count // run
    holders = rows // share
    channels = count * parts
    group = 3 * count

    def body(pieces_ref, out, tall, turned, sems):
        for holder in range(parts):
            for k in range(run):
                at = holder * count + k * share
                start = holder % holders * share
                tall[at : at + share, :] = pieces_ref[
                    holder // holders * run + k, start : start + share, :
                ]
        for tile in range(columns // 128):
            lanes = slice(tile * 128, (tile + 1) * 128)
            turned[lanes, :] = tall[:, lanes].T
        moves = []
        for a in range(3):
            for b in range(3):
                moves.append(
                    pltpu.make_async_copy(
                        turned.at[pl.ds((b * 3 + a) * group, group)],
                        out.at[pl.ds((a * 3 + b) * group, group)],
                        sems.at[a * 3 + b],
                    )
                )
        for move in moves:
            move.start()
        for move in moves:
            move.wait()

    return pl.pallas_call(
        body,
        out_shape=jax.ShapeDtypeStruct((9 * group, channels), pieces.dtype),
        in_specs=[VMEM],
        out_specs=HBM,
        scratch_shapes=[
            pltpu.VMEM((channels, columns), pieces.dtype),
            pltpu.VMEM((columns, channels), pieces.dtype),
            pltpu.SemaphoreType.DMA((9,)),
        ],
        compiler_params=limits(32),
    )(pieces)


def conv_terms(weights, field, mirror, height, breadth, own, up, down):
    count = weights.shape[1] // 9
    places = (down, own, up) if mirror else (up, own, down)
    for a in range(3):
        part = lax.dot_general(
            weights[a],
            field[...],
            (((1,), (0,)), ((), ())),
            preferred_element_type=jnp.float32,
        )
        for q in range(height):
            total = None
            for c in range(3):
                column = None
                for b in range(3):
                    source = q + (1 - b if mirror else b - 1)
                    if 0 <= source < height:
                        at = (b * 3 + c) * count
                        term = part[at : at + count, source * breadth : (source + 1) * breadth]
                        column = term if column is None else column + term
                moved = shift_lanes(column, 1 - c if mirror else c - 1, breadth)
                total = moved if total is None else total + moved
            places[a][:, q * breadth : (q + 1) * breadth] = total


def plane_terms(fore, back, fields, after, height, breadth):
    count = fore.shape[1] // 9
    parts, _, cells = fields.shape

    def body(fore_ref, back_ref, fields_ref, after_ref, own, up, down, vol, cot):
        for part in range(parts):
            rows = pl.ds(part * count, count)
            vol[rows, :] = fields_ref[part, :count, :]
            cot[rows, :] = fields_ref[part, count:, :]
        halves = [pl.ds(0, count), pl.ds(count, count)]
        conv_terms(
            fore_ref, vol, False, height, breadth, *(r.at[halves[0]] for r in (own, up, down))
        )
        conv_terms(
            back_ref, cot, True, height, breadth, *(r.at[halves[1]] for r in (own, up, down))
        )

    shape = jax.ShapeDtypeStruct((2 * count, cells), jnp.float32)
    return pl.pallas_call(
        body,
        out_shape=(shape, shape, shape),
        in_specs=[VMEM, VMEM, VMEM, HBM],
        out_specs=(VMEM, VMEM, VMEM),
        scratch_shapes=[pltpu.VMEM((parts * count, cells), fields.dtype)] * 2,
        compiler_params=limits(12),
        cost_estimate=pl.CostEstimate(
            flops=4 * fore.size * cells,
            bytes_accessed=4 * fore.size + 24 * count * cells,
            transcendentals=0,
        ),
    )(fore, back, fields, after)


def local(volume, kernel, cotangent):
    count, planes, height, breadth = volume.shape
    cells = height * breadth
    channels = kernel.shape[3]
    slabs = lax.axis_size("space")
    parts = lax.axis_size("chan")
    factor = 1.0 / math.sqrt(slabs * planes * cells)
    along_y, near_z, block, far_z = groups_of(slabs)
    up = [(i, i + 1) for i in range(slabs - 1)]
    down = [(i + 1, i) for i in range(slabs - 1)]
    ends = [pair for pair in up if pair[1] % NEAR == 0]
    ends = ends + [(high, low) for low, high in ends]

    cot = flat(cotangent.reshape(count, height, breadth), volume)
    traded = exchange(cot.reshape(NEAR, count // NEAR, cells), "space", near_z)
    vol = flat(volume.reshape(count, height, breadth), cot)
    beyond = lax.ppermute(vol, "space", ends)
    field = lax.all_gather(traded.reshape(count, cells), "chan", axis=0, tiled=True)
    run = exchange(stacked(vol, beyond, NEAR, traded), "space", near_z)

    terms, both = weight_terms(run, field, vol, cot, factor, height, breadth)
    pieces = exchange(terms.reshape(Y_CHIPS, -1, terms.shape[1]), "space", along_y)
    fore, back, ready = own_weights(kernel.reshape(TAPS, channels, channels), count)
    fore = fore.reshape(3, 9 * count, channels)
    back = back.reshape(3, 9 * count, channels)
    fields = lax.all_gather(both, "chan", axis=0)
    total = lax.psum(sum_pieces(pieces, ready), "space", axis_index_groups=far_z)
    whole = exchange(repeated(total, len(block[0]), fields), "space", block)
    weight_grad = in_order(whole, count, parts).reshape(3, 3, 3, count, channels)

    own, upper, lower = plane_terms(fore, back, fields, total, height, breadth)
    from_low = lax.ppermute(upper, "space", up)
    from_high = lax.ppermute(lower, "space", down)
    output, input_grad = finish(own, from_low, from_high, height, breadth, volume.dtype, total)
    return (output.reshape(volume.shape), input_grad.reshape(volume.shape), weight_grad)


def solution(mesh):
    return jax.shard_map(
        local,
        mesh=mesh,
        in_specs=(P("chan", "space", None, None), P(), P("chan", "space", None, None)),
        out_specs=(
            P("chan", "space", None, None),
            P("chan", "space", None, None),
            P(None, None, None, "chan", None),
        ),
        check_vma=False,
    )
```

```python
import math

import jax
import jax.numpy as jnp
from jax import lax
from jax.experimental import pallas as pl
from jax.experimental.pallas import tpu as pltpu
from jax.sharding import PartitionSpec as P

TAPS = 27
Y_CHIPS = 4
NEAR = 4


def groups_of(count):
    length = count // Y_CHIPS
    far = length // NEAR
    block = [
        [y * length + hop * NEAR + k for y in range(Y_CHIPS) for k in range(NEAR)]
        for hop in range(far)
    ]
    far_z = [
        [y * length + hop * NEAR + k for hop in range(far)]
        for y in range(Y_CHIPS)
        for k in range(NEAR)
    ]
    return block, far_z


def exchange(pieces, axis, groups=None):
    return lax.all_to_all(pieces, axis, 0, 0, tiled=True, axis_index_groups=groups)


VMEM = pl.BlockSpec(memory_space=pltpu.VMEM)
HBM = pl.BlockSpec(memory_space=pl.ANY)


def limits(mib=56):
    return pltpu.CompilerParams(vmem_limit_bytes=mib * 1024 * 1024)


TOKEN = jax.ShapeDtypeStruct((8, 128), jnp.float32)


def own_weights(kernel, count):
    channels = kernel.shape[2]
    width = min(channels, 128)
    per = width // count

    def body(kernel_ref, fore, back, token, block, sems):
        token[...] = jnp.zeros(token.shape, token.dtype)
        member = lax.axis_index("chan")
        lanes = pl.ds(pl.multiple_of((member // per) * width, width), width)
        rows = pl.ds(pl.multiple_of(member * count, count), count)
        moves = [
            pltpu.make_async_copy(kernel_ref.at[:, :, lanes], block, sems.at[0]),
            pltpu.make_async_copy(kernel_ref.at[:, rows, :], back, sems.at[1]),
        ]
        for move in moves:
            move.start()
        at = lax.broadcasted_iota(jnp.int32, (count, width), 1)
        row = lax.broadcasted_iota(jnp.int32, (count, width), 0)
        pick = jnp.where(at == row + (member % per) * count, 1.0, 0.0).astype(fore.dtype)
        moves[0].wait()
        for tap in range(TAPS):
            fore[tap] = lax.dot_general(
                pick, block[tap], (((1,), (1,)), ((), ())), preferred_element_type=jnp.float32
            ).astype(fore.dtype)
        moves[1].wait()

    shape = jax.ShapeDtypeStruct((TAPS, count, channels), kernel.dtype)
    return pl.pallas_call(
        body,
        out_shape=(shape, shape, TOKEN),
        in_specs=[HBM],
        out_specs=(VMEM, VMEM, VMEM),
        scratch_shapes=[
            pltpu.VMEM((TAPS, channels, width), kernel.dtype),
            pltpu.SemaphoreType.DMA((2,)),
        ],
        compiler_params=limits(),
    )(kernel)


def spread(block, copies):
    count, height, breadth = block.shape
    cells = height * breadth

    def body(block_ref, out, wide, flat, sems):
        wide[...] = block_ref[...].astype(jnp.float32)
        for q in range(height):
            flat[:, q * breadth : (q + 1) * breadth] = wide[:, q, :].astype(flat.dtype)
        moves = [pltpu.make_async_copy(flat, out.at[k], sems.at[k]) for k in range(copies)]
        for move in moves:
            move.start()
        for move in moves:
            move.wait()

    return pl.pallas_call(
        body,
        out_shape=jax.ShapeDtypeStruct((copies, count, cells), block.dtype),
        in_specs=[VMEM],
        out_specs=HBM,
        scratch_shapes=[
            pltpu.VMEM(block.shape, jnp.float32),
            pltpu.VMEM((count, cells), block.dtype),
            pltpu.SemaphoreType.DMA((copies,)),
        ],
        compiler_params=limits(),
    )(block)


def sum_pieces(pieces, after):
    count, rows, columns = pieces.shape

    def body(pieces_ref, after_ref, out):
        total = pieces_ref[0]
        for k in range(1, count):
            total = total + pieces_ref[k]
        out[...] = total

    return pl.pallas_call(
        body,
        out_shape=jax.ShapeDtypeStruct((rows, columns), pieces.dtype),
        in_specs=[VMEM, VMEM],
        out_specs=VMEM,
        compiler_params=limits(8),
        cost_estimate=pl.CostEstimate(
            flops=pieces.size, bytes_accessed=4 * pieces.size, transcendentals=0
        ),
    )(pieces, after)


def repeated(piece, copies, first, second):
    def body(piece_ref, first_ref, second_ref, out, sems):
        moves = [pltpu.make_async_copy(piece_ref, out.at[k], sems.at[k]) for k in range(copies)]
        for move in moves:
            move.start()
        for move in moves:
            move.wait()

    return pl.pallas_call(
        body,
        out_shape=jax.ShapeDtypeStruct((copies,) + piece.shape, piece.dtype),
        in_specs=[VMEM, HBM, HBM],
        out_specs=HBM,
        scratch_shapes=[pltpu.SemaphoreType.DMA((copies,))],
        compiler_params=limits(32),
    )(piece, first, second)


def finish(own, low, high, height, breadth, dtype, after):
    rows = own.shape[0]
    count = rows // 2

    def body(own_ref, low_ref, high_ref, after_ref, first, second, wide):
        for q in range(height):
            lanes = pl.ds(q * breadth, breadth)
            wide[:, q, :] = own_ref[:, lanes] + low_ref[:, lanes] + high_ref[:, lanes]
        first[...] = wide[:count].astype(dtype)
        second[...] = wide[count:].astype(dtype)

    shape = jax.ShapeDtypeStruct((count, height, breadth), dtype)
    return pl.pallas_call(
        body,
        out_shape=(shape, shape),
        in_specs=[VMEM] * 3 + [HBM],
        out_specs=(VMEM, VMEM),
        scratch_shapes=[pltpu.VMEM((rows, height, breadth), jnp.float32)],
        compiler_params=limits(8),
    )(own, low, high, after)


def shift_lanes(value, offset, lanes):
    if offset == 0:
        return value
    at = lax.broadcasted_iota(jnp.int32, value.shape, 1)
    if offset < 0:
        return jnp.where(at == 0, 0.0, pltpu.roll(value, 1, 1))
    return jnp.where(at == lanes - 1, 0.0, pltpu.roll(value, lanes - 1, 1))


def weight_terms(low, own, high, cot, after, factor, height, breadth):
    count, cells = own.shape
    channels = cot.shape[0]
    group = 3 * count
    rows = 9 * group + count

    def body(low_ref, own_ref, high_ref, cot_ref, after_ref, out, stack, held, out_sems):
        sent = []

        def send(start, size):
            move = pltpu.make_async_copy(
                held.at[pl.ds(start, size)], out.at[pl.ds(start, size)], out_sems.at[len(sent)]
            )
            move.start()
            sent.append(move)

        held[9 * group :, :] = jnp.zeros((count, channels), held.dtype)
        send(9 * group, count)
        edge = jnp.zeros((9 * count, breadth), stack.dtype)
        stack[:, :breadth] = edge
        stack[:, (height + 1) * breadth :] = edge
        for a, plane in enumerate((low_ref, own_ref, high_ref)):
            for q in range(height):
                row = plane[:, q * breadth : (q + 1) * breadth].astype(jnp.float32)
                for c in range(3):
                    at = (a * 3 + c) * count
                    stack[at : at + count, (q + 1) * breadth : (q + 2) * breadth] = shift_lanes(
                        row, c - 1, breadth
                    ).astype(stack.dtype)
        for b in range(3):
            part = lax.dot_general(
                stack[:, b * breadth : b * breadth + cells],
                cot_ref[...],
                (((1,), (1,)), ((), ())),
                preferred_element_type=jnp.float32,
            )
            for a in range(3):
                at = (a * 3 + b) * group
                held[at : at + group, :] = part[a * group : (a + 1) * group] * factor
                send(at, group)
        for move in sent:
            move.wait()

    return pl.pallas_call(
        body,
        out_shape=jax.ShapeDtypeStruct((rows, channels), jnp.float32),
        in_specs=[VMEM] * 5,
        out_specs=HBM,
        scratch_shapes=[
            pltpu.VMEM((9 * count, cells + 2 * breadth), own.dtype),
            pltpu.VMEM((rows, channels), jnp.float32),
            pltpu.SemaphoreType.DMA((10,)),
        ],
        compiler_params=limits(32),
        cost_estimate=pl.CostEstimate(
            flops=2 * rows * channels * cells,
            bytes_accessed=4 * rows * channels,
            transcendentals=0,
        ),
    )(low, own, high, cot, after)


def conv_terms(weights, field, mirror, height, breadth, own, up, down):
    count = weights.shape[1] // 9
    places = (down, own, up) if mirror else (up, own, down)
    for a in range(3):
        part = lax.dot_general(
            weights[a],
            field[...],
            (((1,), (0,)), ((), ())),
            preferred_element_type=jnp.float32,
        )
        for q in range(height):
            total = None
            for c in range(3):
                column = None
                for b in range(3):
                    source = q + (1 - b if mirror else b - 1)
                    if 0 <= source < height:
                        at = (b * 3 + c) * count
                        term = part[at : at + count, source * breadth : (source + 1) * breadth]
                        column = term if column is None else column + term
                moved = shift_lanes(column, 1 - c if mirror else c - 1, breadth)
                total = moved if total is None else total + moved
            places[a][:, q * breadth : (q + 1) * breadth] = total


def plane_terms(fore, vol, back, cot, height, breadth):
    count = fore.shape[1] // 9
    cells = vol.shape[1]

    def body(fore_ref, vol_ref, back_ref, cot_ref, own, up, down, token):
        token[...] = jnp.zeros(token.shape, token.dtype)
        halves = [pl.ds(0, count), pl.ds(count, count)]
        conv_terms(
            fore_ref, vol_ref, False, height, breadth, *(r.at[halves[0]] for r in (own, up, down))
        )
        conv_terms(
            back_ref, cot_ref, True, height, breadth, *(r.at[halves[1]] for r in (own, up, down))
        )

    shape = jax.ShapeDtypeStruct((2 * count, cells), jnp.float32)
    return pl.pallas_call(
        body,
        out_shape=(shape, shape, shape, TOKEN),
        in_specs=[VMEM] * 4,
        out_specs=(VMEM,) * 4,
        compiler_params=limits(12),
        cost_estimate=pl.CostEstimate(
            flops=4 * fore.size * cells,
            bytes_accessed=4 * fore.size + 24 * count * cells,
            transcendentals=0,
        ),
    )(fore, vol, back, cot)


def local(volume, kernel, cotangent):
    count, planes, height, breadth = volume.shape
    cells = height * breadth
    channels = kernel.shape[3]
    slabs = lax.axis_size("space")
    parts = lax.axis_size("chan")
    member = lax.axis_index("chan")
    factor = 1.0 / math.sqrt(slabs * planes * cells)
    block, far_z = groups_of(slabs)
    up = [(i, i + 1) for i in range(slabs - 1)]
    down = [(i + 1, i) for i in range(slabs - 1)]

    cot_copies = spread(cotangent.reshape(count, height, breadth), parts)
    cot_all = exchange(cot_copies, "chan").reshape(channels, cells)
    vol = volume.reshape(count, cells)
    vol_low = lax.ppermute(vol, "space", up)
    vol_high = lax.ppermute(vol, "space", down)
    fore, back, ready = own_weights(kernel.reshape(TAPS, channels, channels), count)
    fore = fore.reshape(3, 9 * count, channels)
    back = back.reshape(3, 9 * count, channels)

    terms = weight_terms(vol_low, vol, vol_high, cot_all, ready, factor, height, breadth)
    pieces = exchange(terms.reshape(len(block[0]), -1, channels), "space", block)
    vol_all = lax.all_gather(vol, "chan", axis=0, tiled=True)
    own, upper, lower, done = plane_terms(fore, vol_all, back, cot_all, height, breadth)
    total = lax.psum(sum_pieces(pieces, done), "space", axis_index_groups=far_z)
    from_low = lax.ppermute(upper, "space", up)
    from_high = lax.ppermute(lower, "space", down)
    copies = repeated(total, len(block[0]), from_low, from_high)
    whole = exchange(copies, "space", block).reshape(-1, channels)
    weight_grad = whole[: TAPS * count].reshape(3, 3, 3, count, channels)

    output, input_grad = finish(own, from_low, from_high, height, breadth, volume.dtype, total)
    return (output.reshape(volume.shape), input_grad.reshape(volume.shape), weight_grad)


def solution(mesh):
    return jax.shard_map(
        local,
        mesh=mesh,
        in_specs=(P("chan", "space", None, None), P(), P("chan", "space", None, None)),
        out_specs=(
            P("chan", "space", None, None),
            P("chan", "space", None, None),
            P(None, None, None, "chan", None),
        ),
        check_vma=False,
    )
```

```python
import math

import jax
import jax.numpy as jnp
from jax import lax
from jax.experimental import pallas as pl
from jax.experimental.pallas import tpu as pltpu
from jax.sharding import PartitionSpec as P

TAPS = 27
Y_CHIPS = 4
NEAR = 4


def groups_of(count):
    length = count // Y_CHIPS
    far = length // NEAR
    block = [
        [y * length + hop * NEAR + k for y in range(Y_CHIPS) for k in range(NEAR)]
        for hop in range(far)
    ]
    far_z = [
        [y * length + hop * NEAR + k for hop in range(far)]
        for y in range(Y_CHIPS)
        for k in range(NEAR)
    ]
    return block, far_z


def exchange(pieces, axis, groups=None):
    return lax.all_to_all(pieces, axis, 0, 0, tiled=True, axis_index_groups=groups)


VMEM = pl.BlockSpec(memory_space=pltpu.VMEM)
HBM = pl.BlockSpec(memory_space=pl.ANY)


def limits(mib=56):
    return pltpu.CompilerParams(vmem_limit_bytes=mib * 1024 * 1024)


TOKEN = jax.ShapeDtypeStruct((1,), jnp.int32)
SMEM = pl.BlockSpec(memory_space=pltpu.SMEM)


def own_weights(kernel, count):
    channels = kernel.shape[2]
    width = min(channels, 128)
    per = width // count

    def body(kernel_ref, fore, back, token, block, sems):
        token[0] = 0
        member = lax.axis_index("chan")
        lanes = pl.ds(pl.multiple_of((member // per) * width, width), width)
        rows = pl.ds(pl.multiple_of(member * count, count), count)
        moves = [
            pltpu.make_async_copy(kernel_ref.at[:, :, lanes], block, sems.at[0]),
            pltpu.make_async_copy(kernel_ref.at[:, rows, :], back, sems.at[1]),
        ]
        for move in moves:
            move.start()
        at = lax.broadcasted_iota(jnp.int32, (count, width), 1)
        row = lax.broadcasted_iota(jnp.int32, (count, width), 0)
        pick = jnp.where(at == row + (member % per) * count, 1.0, 0.0).astype(fore.dtype)
        moves[0].wait()
        for tap in range(TAPS):
            fore[tap] = lax.dot_general(
                pick, block[tap], (((1,), (1,)), ((), ())), preferred_element_type=jnp.float32
            ).astype(fore.dtype)
        moves[1].wait()

    shape = jax.ShapeDtypeStruct((TAPS, count, channels), kernel.dtype)
    return pl.pallas_call(
        body,
        out_shape=(shape, shape, TOKEN),
        in_specs=[HBM],
        out_specs=(VMEM, VMEM, SMEM),
        scratch_shapes=[
            pltpu.VMEM((TAPS, channels, width), kernel.dtype),
            pltpu.SemaphoreType.DMA((2,)),
        ],
        compiler_params=limits(),
    )(kernel)


def spread(block, copies):
    count, height, breadth = block.shape
    cells = height * breadth

    def body(block_ref, out, wide, flat, sems):
        wide[...] = block_ref[...].astype(jnp.float32)
        for q in range(height):
            flat[:, q * breadth : (q + 1) * breadth] = wide[:, q, :].astype(flat.dtype)
        moves = [pltpu.make_async_copy(flat, out.at[k], sems.at[k]) for k in range(copies)]
        for move in moves:
            move.start()
        for move in moves:
            move.wait()

    return pl.pallas_call(
        body,
        out_shape=jax.ShapeDtypeStruct((copies, count, cells), block.dtype),
        in_specs=[VMEM],
        out_specs=HBM,
        scratch_shapes=[
            pltpu.VMEM(block.shape, jnp.float32),
            pltpu.VMEM((count, cells), block.dtype),
            pltpu.SemaphoreType.DMA((copies,)),
        ],
        compiler_params=limits(),
    )(block)


def sum_pieces(pieces, after):
    count, rows, columns = pieces.shape

    def body(pieces_ref, after_ref, out):
        total = pieces_ref[0]
        for k in range(1, count):
            total = total + pieces_ref[k]
        out[...] = total

    return pl.pallas_call(
        body,
        out_shape=jax.ShapeDtypeStruct((rows, columns), pieces.dtype),
        in_specs=[VMEM, SMEM],
        out_specs=VMEM,
        compiler_params=limits(8),
        cost_estimate=pl.CostEstimate(
            flops=pieces.size, bytes_accessed=4 * pieces.size, transcendentals=0
        ),
    )(pieces, after)


TOP = 13.0
SPARE = 8


def scaled(piece, first, second):
    rows, columns = piece.shape

    def body(piece_ref, first_ref, second_ref, out):
        value = piece_ref[...]
        most = jnp.max(jnp.max(jnp.abs(value), axis=0, keepdims=True), axis=1, keepdims=True)
        power = jnp.floor(jnp.log2(jnp.maximum(most, 1e-34)))
        out[:rows, :] = value * jnp.exp2(TOP - power)
        out[rows:, :] = jnp.broadcast_to(power, (SPARE, columns))

    return pl.pallas_call(
        body,
        out_shape=jax.ShapeDtypeStruct((rows + SPARE, columns), piece.dtype),
        in_specs=[VMEM, HBM, HBM],
        out_specs=VMEM,
        compiler_params=limits(32),
    )(piece, first, second)


def unscaled(pieces, amount):
    count, height, columns = pieces.shape
    rows = height - SPARE
    spans = [(k * rows, min(rows, amount - k * rows)) for k in range(count) if k * rows < amount]

    def body(pieces_ref, out, held, sems):
        moves = []
        for k, (start, size) in enumerate(spans):
            power = pieces_ref[k, rows:, :][:1]
            held[start : start + size, :] = pieces_ref[k, :size, :] * jnp.exp2(power - TOP)
            span = pl.ds(start, size)
            moves.append(pltpu.make_async_copy(held.at[span], out.at[span], sems.at[k]))
            moves[-1].start()
        for move in moves:
            move.wait()

    return pl.pallas_call(
        body,
        out_shape=jax.ShapeDtypeStruct((amount, columns), pieces.dtype),
        in_specs=[VMEM],
        out_specs=HBM,
        scratch_shapes=[
            pltpu.VMEM((amount, columns), pieces.dtype),
            pltpu.SemaphoreType.DMA((len(spans),)),
        ],
        compiler_params=limits(32),
    )(pieces)


def finish(own, low, high, height, breadth, dtype, after):
    rows = own.shape[0]
    count = rows // 2

    def body(own_ref, low_ref, high_ref, after_ref, first, second, wide):
        for q in range(height):
            lanes = pl.ds(q * breadth, breadth)
            wide[:, q, :] = own_ref[:, lanes] + low_ref[:, lanes] + high_ref[:, lanes]
        first[...] = wide[:count].astype(dtype)
        second[...] = wide[count:].astype(dtype)

    shape = jax.ShapeDtypeStruct((count, height, breadth), dtype)
    return pl.pallas_call(
        body,
        out_shape=(shape, shape),
        in_specs=[VMEM] * 3 + [HBM],
        out_specs=(VMEM, VMEM),
        scratch_shapes=[pltpu.VMEM((rows, height, breadth), jnp.float32)],
        compiler_params=limits(8),
    )(own, low, high, after)


def shift_lanes(value, offset, lanes):
    if offset == 0:
        return value
    at = lax.broadcasted_iota(jnp.int32, value.shape, 1)
    if offset < 0:
        return jnp.where(at == 0, 0.0, pltpu.roll(value, 1, 1))
    return jnp.where(at == lanes - 1, 0.0, pltpu.roll(value, lanes - 1, 1))


def weight_terms(low, own, high, cot, after, factor, height, breadth):
    count, cells = own.shape
    channels = cot.shape[0]
    group = 3 * count
    rows = 9 * group + count

    def body(low_ref, own_ref, high_ref, cot_ref, after_ref, out, stack, held, out_sems):
        sent = []

        def send(start, size):
            move = pltpu.make_async_copy(
                held.at[pl.ds(start, size)], out.at[pl.ds(start, size)], out_sems.at[len(sent)]
            )
            move.start()
            sent.append(move)

        held[9 * group :, :] = jnp.zeros((count, channels), held.dtype)
        send(9 * group, count)
        edge = jnp.zeros((9 * count, breadth), stack.dtype)
        stack[:, :breadth] = edge
        stack[:, (height + 1) * breadth :] = edge
        for a, plane in enumerate((low_ref, own_ref, high_ref)):
            for q in range(height):
                row = plane[:, q * breadth : (q + 1) * breadth].astype(jnp.float32)
                for c in range(3):
                    at = (a * 3 + c) * count
                    stack[at : at + count, (q + 1) * breadth : (q + 2) * breadth] = shift_lanes(
                        row, c - 1, breadth
                    ).astype(stack.dtype)
        for b in range(3):
            part = lax.dot_general(
                stack[:, b * breadth : b * breadth + cells],
                cot_ref[...],
                (((1,), (1,)), ((), ())),
                preferred_element_type=jnp.float32,
            )
            for a in range(3):
                at = (a * 3 + b) * group
                held[at : at + group, :] = part[a * group : (a + 1) * group] * factor
                send(at, group)
        for move in sent:
            move.wait()

    return pl.pallas_call(
        body,
        out_shape=jax.ShapeDtypeStruct((rows, channels), jnp.float32),
        in_specs=[VMEM] * 4 + [SMEM],
        out_specs=HBM,
        scratch_shapes=[
            pltpu.VMEM((9 * count, cells + 2 * breadth), own.dtype),
            pltpu.VMEM((rows, channels), jnp.float32),
            pltpu.SemaphoreType.DMA((10,)),
        ],
        compiler_params=limits(32),
        cost_estimate=pl.CostEstimate(
            flops=2 * rows * channels * cells,
            bytes_accessed=4 * rows * channels,
            transcendentals=0,
        ),
    )(low, own, high, cot, after)


def conv_terms(weights, field, mirror, height, breadth, own, up, down):
    count = weights.shape[1] // 9
    places = (down, own, up) if mirror else (up, own, down)
    for a in range(3):
        part = lax.dot_general(
            weights[a],
            field[...],
            (((1,), (0,)), ((), ())),
            preferred_element_type=jnp.float32,
        )
        for q in range(height):
            total = None
            for c in range(3):
                column = None
                for b in range(3):
                    source = q + (1 - b if mirror else b - 1)
                    if 0 <= source < height:
                        at = (b * 3 + c) * count
                        term = part[at : at + count, source * breadth : (source + 1) * breadth]
                        column = term if column is None else column + term
                moved = shift_lanes(column, 1 - c if mirror else c - 1, breadth)
                total = moved if total is None else total + moved
            places[a][:, q * breadth : (q + 1) * breadth] = total


def plane_terms(fore, vol, back, cot, height, breadth):
    count = fore.shape[1] // 9
    cells = vol.shape[1]

    def body(fore_ref, vol_ref, back_ref, cot_ref, own, up, down, token):
        token[0] = 0
        halves = [pl.ds(0, count), pl.ds(count, count)]
        conv_terms(
            fore_ref, vol_ref, False, height, breadth, *(r.at[halves[0]] for r in (own, up, down))
        )
        conv_terms(
            back_ref, cot_ref, True, height, breadth, *(r.at[halves[1]] for r in (own, up, down))
        )

    shape = jax.ShapeDtypeStruct((2 * count, cells), jnp.float32)
    return pl.pallas_call(
        body,
        out_shape=(shape, shape, shape, TOKEN),
        in_specs=[VMEM] * 4,
        out_specs=(VMEM, VMEM, VMEM, SMEM),
        compiler_params=limits(12),
        cost_estimate=pl.CostEstimate(
            flops=4 * fore.size * cells,
            bytes_accessed=4 * fore.size + 24 * count * cells,
            transcendentals=0,
        ),
    )(fore, vol, back, cot)


def local(volume, kernel, cotangent):
    count, planes, height, breadth = volume.shape
    cells = height * breadth
    channels = kernel.shape[3]
    slabs = lax.axis_size("space")
    parts = lax.axis_size("chan")
    member = lax.axis_index("chan")
    factor = 1.0 / math.sqrt(slabs * planes * cells)
    block, far_z = groups_of(slabs)
    up = [(i, i + 1) for i in range(slabs - 1)]
    down = [(i + 1, i) for i in range(slabs - 1)]

    cot_copies = spread(cotangent.reshape(count, height, breadth), parts)
    cot_all = exchange(cot_copies, "chan").reshape(channels, cells)
    vol = volume.reshape(count, cells)
    vol_low = lax.ppermute(vol, "space", up)
    vol_high = lax.ppermute(vol, "space", down)
    fore, back, ready = own_weights(kernel.reshape(TAPS, channels, channels), count)
    fore = fore.reshape(3, 9 * count, channels)
    back = back.reshape(3, 9 * count, channels)

    terms = weight_terms(vol_low, vol, vol_high, cot_all, ready, factor, height, breadth)
    pieces = exchange(terms.reshape(len(block[0]), -1, channels), "space", block)
    vol_all = lax.all_gather(vol, "chan", axis=0, tiled=True)
    own, upper, lower, done = plane_terms(fore, vol_all, back, cot_all, height, breadth)
    total = lax.psum(sum_pieces(pieces, done), "space", axis_index_groups=far_z)
    from_low = lax.ppermute(upper, "space", up)
    from_high = lax.ppermute(lower, "space", down)
    packed = scaled(total, from_low, from_high).astype(jnp.float16)
    copies = jnp.broadcast_to(packed[None], (len(block[0]),) + packed.shape)
    whole = exchange(copies, "space", block).astype(jnp.float32)
    weight_grad = unscaled(whole, TAPS * count).reshape(3, 3, 3, count, channels)

    output, input_grad = finish(own, from_low, from_high, height, breadth, volume.dtype, total)
    return (output.reshape(volume.shape), input_grad.reshape(volume.shape), weight_grad)


def solution(mesh):
    return jax.shard_map(
        local,
        mesh=mesh,
        in_specs=(P("chan", "space", None, None), P(), P("chan", "space", None, None)),
        out_specs=(
            P("chan", "space", None, None),
            P("chan", "space", None, None),
            P(None, None, None, "chan", None),
        ),
        check_vma=False,
    )
```

```python
import math

import jax
import jax.numpy as jnp
from jax import lax
from jax.experimental import pallas as pl
from jax.experimental.pallas import tpu as pltpu
from jax.sharding import PartitionSpec as P

TAPS = 27
Y_CHIPS = 4
NEAR = 4


def groups_of(count):
    length = count // Y_CHIPS
    far = length // NEAR
    block = [
        [y * length + hop * NEAR + k for y in range(Y_CHIPS) for k in range(NEAR)]
        for hop in range(far)
    ]
    far_z = [
        [y * length + hop * NEAR + k for hop in range(far)]
        for y in range(Y_CHIPS)
        for k in range(NEAR)
    ]
    return block, far_z


def exchange(pieces, axis, groups=None):
    return lax.all_to_all(pieces, axis, 0, 0, tiled=True, axis_index_groups=groups)


VMEM = pl.BlockSpec(memory_space=pltpu.VMEM)
HBM = pl.BlockSpec(memory_space=pl.ANY)


def limits(mib=56):
    return pltpu.CompilerParams(vmem_limit_bytes=mib * 1024 * 1024)


TOKEN = jax.ShapeDtypeStruct((1,), jnp.int32)
SMEM = pl.BlockSpec(memory_space=pltpu.SMEM)


def own_weights(kernel, count):
    channels = kernel.shape[2]
    width = min(channels, 128)
    per = width // count

    def body(kernel_ref, fore, back, token, block, sems):
        token[0] = 0
        member = lax.axis_index("chan")
        lanes = pl.ds(pl.multiple_of((member // per) * width, width), width)
        rows = pl.ds(pl.multiple_of(member * count, count), count)
        moves = [
            pltpu.make_async_copy(kernel_ref.at[:, :, lanes], block, sems.at[0]),
            pltpu.make_async_copy(kernel_ref.at[:, rows, :], back, sems.at[1]),
        ]
        for move in moves:
            move.start()
        at = lax.broadcasted_iota(jnp.int32, (count, width), 1)
        row = lax.broadcasted_iota(jnp.int32, (count, width), 0)
        pick = jnp.where(at == row + (member % per) * count, 1.0, 0.0).astype(fore.dtype)
        moves[0].wait()
        for tap in range(TAPS):
            fore[tap] = lax.dot_general(
                pick, block[tap], (((1,), (1,)), ((), ())), preferred_element_type=jnp.float32
            ).astype(fore.dtype)
        moves[1].wait()

    shape = jax.ShapeDtypeStruct((TAPS, count, channels), kernel.dtype)
    return pl.pallas_call(
        body,
        out_shape=(shape, shape, TOKEN),
        in_specs=[HBM],
        out_specs=(VMEM, VMEM, SMEM),
        scratch_shapes=[
            pltpu.VMEM((TAPS, channels, width), kernel.dtype),
            pltpu.SemaphoreType.DMA((2,)),
        ],
        compiler_params=limits(),
    )(kernel)


def spread(block, copies):
    count, height, breadth = block.shape
    cells = height * breadth

    def body(block_ref, out, wide, flat, sems):
        wide[...] = block_ref[...].astype(jnp.float32)
        for q in range(height):
            flat[:, q * breadth : (q + 1) * breadth] = wide[:, q, :].astype(flat.dtype)
        moves = [pltpu.make_async_copy(flat, out.at[k], sems.at[k]) for k in range(copies)]
        for move in moves:
            move.start()
        for move in moves:
            move.wait()

    return pl.pallas_call(
        body,
        out_shape=jax.ShapeDtypeStruct((copies, count, cells), block.dtype),
        in_specs=[VMEM],
        out_specs=HBM,
        scratch_shapes=[
            pltpu.VMEM(block.shape, jnp.float32),
            pltpu.VMEM((count, cells), block.dtype),
            pltpu.SemaphoreType.DMA((copies,)),
        ],
        compiler_params=limits(),
    )(block)


def sum_pieces(pieces, after):
    count, rows, columns = pieces.shape

    def body(pieces_ref, after_ref, out):
        total = pieces_ref[0]
        for k in range(1, count):
            total = total + pieces_ref[k]
        out[...] = total

    return pl.pallas_call(
        body,
        out_shape=jax.ShapeDtypeStruct((rows, columns), pieces.dtype),
        in_specs=[VMEM, SMEM],
        out_specs=VMEM,
        compiler_params=limits(8),
        cost_estimate=pl.CostEstimate(
            flops=pieces.size, bytes_accessed=4 * pieces.size, transcendentals=0
        ),
    )(pieces, after)


TOP = 13.0
SPARE = 8


def scaled(pieces, first, second):
    count, rows, columns = pieces.shape

    def body(pieces_ref, first_ref, second_ref, out):
        value = pieces_ref[0]
        for k in range(1, count):
            value = value + pieces_ref[k]
        most = jnp.max(jnp.max(jnp.abs(value), axis=0, keepdims=True), axis=1, keepdims=True)
        power = jnp.floor(jnp.log2(jnp.maximum(most, 1e-34)))
        out[:rows, :] = value * jnp.exp2(TOP - power)
        out[rows:, :] = jnp.broadcast_to(power, (SPARE, columns))

    return pl.pallas_call(
        body,
        out_shape=jax.ShapeDtypeStruct((rows + SPARE, columns), pieces.dtype),
        in_specs=[VMEM, HBM, HBM],
        out_specs=VMEM,
        compiler_params=limits(32),
    )(pieces, first, second)


def unscaled(pieces, amount):
    count, height, columns = pieces.shape
    rows = height - SPARE
    spans = [(k * rows, min(rows, amount - k * rows)) for k in range(count) if k * rows < amount]

    def body(pieces_ref, out, held, sems):
        moves = []
        for k, (start, size) in enumerate(spans):
            power = pieces_ref[k, rows:, :][:1]
            held[start : start + size, :] = pieces_ref[k, :size, :] * jnp.exp2(power - TOP)
            span = pl.ds(start, size)
            moves.append(pltpu.make_async_copy(held.at[span], out.at[span], sems.at[k]))
            moves[-1].start()
        for move in moves:
            move.wait()

    return pl.pallas_call(
        body,
        out_shape=jax.ShapeDtypeStruct((amount, columns), pieces.dtype),
        in_specs=[VMEM],
        out_specs=HBM,
        scratch_shapes=[
            pltpu.VMEM((amount, columns), pieces.dtype),
            pltpu.SemaphoreType.DMA((len(spans),)),
        ],
        compiler_params=limits(32),
    )(pieces)


def finish(own, low, high, height, breadth, dtype, after):
    rows = own.shape[0]
    count = rows // 2

    def body(own_ref, low_ref, high_ref, after_ref, first, second, wide):
        for q in range(height):
            lanes = pl.ds(q * breadth, breadth)
            wide[:, q, :] = own_ref[:, lanes] + low_ref[:, lanes] + high_ref[:, lanes]
        first[...] = wide[:count].astype(dtype)
        second[...] = wide[count:].astype(dtype)

    shape = jax.ShapeDtypeStruct((count, height, breadth), dtype)
    return pl.pallas_call(
        body,
        out_shape=(shape, shape),
        in_specs=[VMEM] * 3 + [HBM],
        out_specs=(VMEM, VMEM),
        scratch_shapes=[pltpu.VMEM((rows, height, breadth), jnp.float32)],
        compiler_params=limits(8),
    )(own, low, high, after)


def shift_lanes(value, offset, lanes):
    if offset == 0:
        return value
    at = lax.broadcasted_iota(jnp.int32, value.shape, 1)
    if offset < 0:
        return jnp.where(at == 0, 0.0, pltpu.roll(value, 1, 1))
    return jnp.where(at == lanes - 1, 0.0, pltpu.roll(value, lanes - 1, 1))


def weight_terms(low, own, high, cot, after, factor, height, breadth):
    count, cells = own.shape
    channels = cot.shape[0]
    group = 3 * count
    rows = 9 * group + count

    def body(low_ref, own_ref, high_ref, cot_ref, after_ref, out, stack, held, out_sems):
        sent = []

        def send(start, size):
            move = pltpu.make_async_copy(
                held.at[pl.ds(start, size)], out.at[pl.ds(start, size)], out_sems.at[len(sent)]
            )
            move.start()
            sent.append(move)

        held[9 * group :, :] = jnp.zeros((count, channels), held.dtype)
        send(9 * group, count)
        edge = jnp.zeros((9 * count, breadth), stack.dtype)
        stack[:, :breadth] = edge
        stack[:, (height + 1) * breadth :] = edge
        for a, plane in enumerate((low_ref, own_ref, high_ref)):
            for q in range(height):
                row = plane[:, q * breadth : (q + 1) * breadth].astype(jnp.float32)
                for c in range(3):
                    at = (a * 3 + c) * count
                    stack[at : at + count, (q + 1) * breadth : (q + 2) * breadth] = shift_lanes(
                        row, c - 1, breadth
                    ).astype(stack.dtype)
        for b in range(3):
            part = lax.dot_general(
                stack[:, b * breadth : b * breadth + cells],
                cot_ref[...],
                (((1,), (1,)), ((), ())),
                preferred_element_type=jnp.float32,
            )
            for a in range(3):
                at = (a * 3 + b) * group
                held[at : at + group, :] = part[a * group : (a + 1) * group] * factor
                send(at, group)
        for move in sent:
            move.wait()

    return pl.pallas_call(
        body,
        out_shape=jax.ShapeDtypeStruct((rows, channels), jnp.float32),
        in_specs=[VMEM] * 4 + [SMEM],
        out_specs=HBM,
        scratch_shapes=[
            pltpu.VMEM((9 * count, cells + 2 * breadth), own.dtype),
            pltpu.VMEM((rows, channels), jnp.float32),
            pltpu.SemaphoreType.DMA((10,)),
        ],
        compiler_params=limits(32),
        cost_estimate=pl.CostEstimate(
            flops=2 * rows * channels * cells,
            bytes_accessed=4 * rows * channels,
            transcendentals=0,
        ),
    )(low, own, high, cot, after)


def conv_terms(weights, field, mirror, height, breadth, own, up, down):
    count = weights.shape[1] // 9
    places = (down, own, up) if mirror else (up, own, down)
    for a in range(3):
        part = lax.dot_general(
            weights[a],
            field[...],
            (((1,), (0,)), ((), ())),
            preferred_element_type=jnp.float32,
        )
        for q in range(height):
            total = None
            for c in range(3):
                column = None
                for b in range(3):
                    source = q + (1 - b if mirror else b - 1)
                    if 0 <= source < height:
                        at = (b * 3 + c) * count
                        term = part[at : at + count, source * breadth : (source + 1) * breadth]
                        column = term if column is None else column + term
                moved = shift_lanes(column, 1 - c if mirror else c - 1, breadth)
                total = moved if total is None else total + moved
            places[a][:, q * breadth : (q + 1) * breadth] = total


def plane_terms(fore, vol, back, cot, height, breadth):
    count = fore.shape[1] // 9
    cells = vol.shape[1]

    def body(fore_ref, vol_ref, back_ref, cot_ref, own, up, down, token):
        token[0] = 0
        halves = [pl.ds(0, count), pl.ds(count, count)]
        conv_terms(
            fore_ref, vol_ref, False, height, breadth, *(r.at[halves[0]] for r in (own, up, down))
        )
        conv_terms(
            back_ref, cot_ref, True, height, breadth, *(r.at[halves[1]] for r in (own, up, down))
        )

    shape = jax.ShapeDtypeStruct((2 * count, cells), jnp.float32)
    return pl.pallas_call(
        body,
        out_shape=(shape, shape, shape, TOKEN),
        in_specs=[VMEM] * 4,
        out_specs=(VMEM, VMEM, VMEM, SMEM),
        compiler_params=limits(12),
        cost_estimate=pl.CostEstimate(
            flops=4 * fore.size * cells,
            bytes_accessed=4 * fore.size + 24 * count * cells,
            transcendentals=0,
        ),
    )(fore, vol, back, cot)


def local(volume, kernel, cotangent):
    count, planes, height, breadth = volume.shape
    cells = height * breadth
    channels = kernel.shape[3]
    slabs = lax.axis_size("space")
    parts = lax.axis_size("chan")
    member = lax.axis_index("chan")
    factor = 1.0 / math.sqrt(slabs * planes * cells)
    block, far_z = groups_of(slabs)
    up = [(i, i + 1) for i in range(slabs - 1)]
    down = [(i + 1, i) for i in range(slabs - 1)]

    cot_copies = spread(cotangent.reshape(count, height, breadth), parts)
    cot_all = exchange(cot_copies, "chan").reshape(channels, cells)
    vol = volume.reshape(count, cells)
    vol_low = lax.ppermute(vol, "space", up)
    vol_high = lax.ppermute(vol, "space", down)
    fore, back, ready = own_weights(kernel.reshape(TAPS, channels, channels), count)
    fore = fore.reshape(3, 9 * count, channels)
    back = back.reshape(3, 9 * count, channels)

    terms = weight_terms(vol_low, vol, vol_high, cot_all, ready, factor, height, breadth)
    pieces = exchange(terms.reshape(len(block[0]), -1, channels), "space", block)
    vol_all = lax.all_gather(vol, "chan", axis=0, tiled=True)
    own, upper, lower, done = plane_terms(fore, vol_all, back, cot_all, height, breadth)
    near = sum_pieces(pieces, done)
    far = lax.all_gather(near, "space", axis=0, axis_index_groups=far_z)
    from_low = lax.ppermute(upper, "space", up)
    from_high = lax.ppermute(lower, "space", down)
    packed = scaled(far, from_low, from_high).astype(jnp.float16)
    copies = jnp.broadcast_to(packed[None], (len(block[0]),) + packed.shape)
    whole = exchange(copies, "space", block).astype(jnp.float32)
    weight_grad = unscaled(whole, TAPS * count).reshape(3, 3, 3, count, channels)

    output, input_grad = finish(own, from_low, from_high, height, breadth, volume.dtype, far)
    return (output.reshape(volume.shape), input_grad.reshape(volume.shape), weight_grad)


def solution(mesh):
    return jax.shard_map(
        local,
        mesh=mesh,
        in_specs=(P("chan", "space", None, None), P(), P("chan", "space", None, None)),
        out_specs=(
            P("chan", "space", None, None),
            P("chan", "space", None, None),
            P(None, None, None, "chan", None),
        ),
        check_vma=False,
    )
```

```python
import math

import jax
import jax.numpy as jnp
from jax import lax
from jax.experimental import pallas as pl
from jax.experimental.pallas import tpu as pltpu
from jax.sharding import PartitionSpec as P

TAPS = 27
Y_CHIPS = 4
NEAR = 4


def groups_of(count):
    length = count // Y_CHIPS
    far = length // NEAR
    along_y = [[y * length + z for y in range(Y_CHIPS)] for z in range(length)]
    near_z = [[hop * NEAR + k for k in range(NEAR)] for hop in range(count // NEAR)]
    block = [
        [y * length + hop * NEAR + k for y in range(Y_CHIPS) for k in range(NEAR)]
        for hop in range(far)
    ]
    far_z = [
        [y * length + hop * NEAR + k for hop in range(far)]
        for y in range(Y_CHIPS)
        for k in range(NEAR)
    ]
    return along_y, near_z, block, far_z


def exchange(pieces, axis, groups=None):
    return lax.all_to_all(pieces, axis, 0, 0, tiled=True, axis_index_groups=groups)


VMEM = pl.BlockSpec(memory_space=pltpu.VMEM)
HBM = pl.BlockSpec(memory_space=pl.ANY)


def limits(mib=56):
    return pltpu.CompilerParams(vmem_limit_bytes=mib * 1024 * 1024)


TOKEN = jax.ShapeDtypeStruct((1,), jnp.int32)
SMEM = pl.BlockSpec(memory_space=pltpu.SMEM)


def own_weights(kernel, count):
    channels = kernel.shape[2]
    width = min(channels, 128)
    per = width // count

    def body(kernel_ref, fore, back, token, block, sems):
        token[0] = 0
        member = lax.axis_index("chan")
        lanes = pl.ds(pl.multiple_of((member // per) * width, width), width)
        rows = pl.ds(pl.multiple_of(member * count, count), count)
        moves = [
            pltpu.make_async_copy(kernel_ref.at[:, :, lanes], block, sems.at[0]),
            pltpu.make_async_copy(kernel_ref.at[:, rows, :], back, sems.at[1]),
        ]
        for move in moves:
            move.start()
        at = lax.broadcasted_iota(jnp.int32, (count, width), 1)
        row = lax.broadcasted_iota(jnp.int32, (count, width), 0)
        pick = jnp.where(at == row + (member % per) * count, 1.0, 0.0).astype(fore.dtype)
        moves[0].wait()
        for tap in range(TAPS):
            fore[tap] = lax.dot_general(
                pick, block[tap], (((1,), (1,)), ((), ())), preferred_element_type=jnp.float32
            ).astype(fore.dtype)
        moves[1].wait()

    shape = jax.ShapeDtypeStruct((TAPS, count, channels), kernel.dtype)
    return pl.pallas_call(
        body,
        out_shape=(shape, shape, TOKEN),
        in_specs=[HBM],
        out_specs=(VMEM, VMEM, SMEM),
        scratch_shapes=[
            pltpu.VMEM((TAPS, channels, width), kernel.dtype),
            pltpu.SemaphoreType.DMA((2,)),
        ],
        compiler_params=limits(),
    )(kernel)


def spread(block, copies):
    count, height, breadth = block.shape
    cells = height * breadth

    def body(block_ref, out, wide, flat, sems):
        wide[...] = block_ref[...].astype(jnp.float32)
        for q in range(height):
            flat[:, q * breadth : (q + 1) * breadth] = wide[:, q, :].astype(flat.dtype)
        moves = [pltpu.make_async_copy(flat, out.at[k], sems.at[k]) for k in range(copies)]
        for move in moves:
            move.start()
        for move in moves:
            move.wait()

    return pl.pallas_call(
        body,
        out_shape=jax.ShapeDtypeStruct((copies, count, cells), block.dtype),
        in_specs=[VMEM],
        out_specs=HBM,
        scratch_shapes=[
            pltpu.VMEM(block.shape, jnp.float32),
            pltpu.VMEM((count, cells), block.dtype),
            pltpu.SemaphoreType.DMA((copies,)),
        ],
        compiler_params=limits(),
    )(block)


def sum_pieces(pieces, after):
    count, rows, columns = pieces.shape

    def body(pieces_ref, after_ref, out):
        total = pieces_ref[0]
        for k in range(1, count):
            total = total + pieces_ref[k]
        out[...] = total

    return pl.pallas_call(
        body,
        out_shape=jax.ShapeDtypeStruct((rows, columns), pieces.dtype),
        in_specs=[VMEM, pl.BlockSpec(memory_space=pl.ANY)],
        out_specs=VMEM,
        compiler_params=limits(8),
        cost_estimate=pl.CostEstimate(
            flops=pieces.size, bytes_accessed=4 * pieces.size, transcendentals=0
        ),
    )(pieces, after)


TOP = 13.0
SPARE = 8


def scaled(pieces, first, second):
    count, rows, columns = pieces.shape

    def body(pieces_ref, first_ref, second_ref, out):
        value = pieces_ref[0]
        for k in range(1, count):
            value = value + pieces_ref[k]
        most = jnp.max(jnp.max(jnp.abs(value), axis=0, keepdims=True), axis=1, keepdims=True)
        power = jnp.floor(jnp.log2(jnp.maximum(most, 1e-34)))
        out[:rows, :] = value * jnp.exp2(TOP - power)
        out[rows:, :] = jnp.broadcast_to(power, (SPARE, columns))

    return pl.pallas_call(
        body,
        out_shape=jax.ShapeDtypeStruct((rows + SPARE, columns), pieces.dtype),
        in_specs=[VMEM, HBM, HBM],
        out_specs=VMEM,
        compiler_params=limits(32),
    )(pieces, first, second)


def unscaled(pieces, amount):
    count, height, columns = pieces.shape
    rows = height - SPARE
    spans = [(k * rows, min(rows, amount - k * rows)) for k in range(count) if k * rows < amount]

    def body(pieces_ref, out, held, sems):
        moves = []
        for k, (start, size) in enumerate(spans):
            power = pieces_ref[k, rows:, :][:1]
            held[start : start + size, :] = pieces_ref[k, :size, :] * jnp.exp2(power - TOP)
            span = pl.ds(start, size)
            moves.append(pltpu.make_async_copy(held.at[span], out.at[span], sems.at[k]))
            moves[-1].start()
        for move in moves:
            move.wait()

    return pl.pallas_call(
        body,
        out_shape=jax.ShapeDtypeStruct((amount, columns), pieces.dtype),
        in_specs=[VMEM],
        out_specs=HBM,
        scratch_shapes=[
            pltpu.VMEM((amount, columns), pieces.dtype),
            pltpu.SemaphoreType.DMA((len(spans),)),
        ],
        compiler_params=limits(32),
    )(pieces)


def finish(own, low, high, height, breadth, dtype, after):
    rows = own.shape[0]
    count = rows // 2

    def body(own_ref, low_ref, high_ref, after_ref, first, second, wide):
        for q in range(height):
            lanes = pl.ds(q * breadth, breadth)
            wide[:, q, :] = own_ref[:, lanes] + low_ref[:, lanes] + high_ref[:, lanes]
        first[...] = wide[:count].astype(dtype)
        second[...] = wide[count:].astype(dtype)

    shape = jax.ShapeDtypeStruct((count, height, breadth), dtype)
    return pl.pallas_call(
        body,
        out_shape=(shape, shape),
        in_specs=[VMEM] * 3 + [HBM],
        out_specs=(VMEM, VMEM),
        scratch_shapes=[pltpu.VMEM((rows, height, breadth), jnp.float32)],
        compiler_params=limits(8),
    )(own, low, high, after)


def shift_lanes(value, offset, lanes):
    if offset == 0:
        return value
    at = lax.broadcasted_iota(jnp.int32, value.shape, 1)
    if offset < 0:
        return jnp.where(at == 0, 0.0, pltpu.roll(value, 1, 1))
    return jnp.where(at == lanes - 1, 0.0, pltpu.roll(value, lanes - 1, 1))


def weight_terms(low, own, high, cot, after, factor, height, breadth):
    count, cells = own.shape
    channels = cot.shape[0]
    group = 3 * count
    rows = 9 * group + count

    def body(low_ref, own_ref, high_ref, cot_ref, after_ref, out, stack, held, out_sems):
        sent = []

        def send(start, size):
            move = pltpu.make_async_copy(
                held.at[pl.ds(start, size)], out.at[pl.ds(start, size)], out_sems.at[len(sent)]
            )
            move.start()
            sent.append(move)

        held[9 * group :, :] = jnp.zeros((count, channels), held.dtype)
        send(9 * group, count)
        edge = jnp.zeros((9 * count, breadth), stack.dtype)
        stack[:, :breadth] = edge
        stack[:, (height + 1) * breadth :] = edge
        for a, plane in enumerate((low_ref, own_ref, high_ref)):
            for q in range(height):
                row = plane[:, q * breadth : (q + 1) * breadth].astype(jnp.float32)
                for c in range(3):
                    at = (a * 3 + c) * count
                    stack[at : at + count, (q + 1) * breadth : (q + 2) * breadth] = shift_lanes(
                        row, c - 1, breadth
                    ).astype(stack.dtype)
        for b in range(3):
            part = lax.dot_general(
                stack[:, b * breadth : b * breadth + cells],
                cot_ref[...],
                (((1,), (1,)), ((), ())),
                preferred_element_type=jnp.float32,
            )
            for a in range(3):
                at = (a * 3 + b) * group
                held[at : at + group, :] = part[a * group : (a + 1) * group] * factor
                send(at, group)
        for move in sent:
            move.wait()

    return pl.pallas_call(
        body,
        out_shape=jax.ShapeDtypeStruct((rows, channels), jnp.float32),
        in_specs=[VMEM] * 4 + [SMEM],
        out_specs=HBM,
        scratch_shapes=[
            pltpu.VMEM((9 * count, cells + 2 * breadth), own.dtype),
            pltpu.VMEM((rows, channels), jnp.float32),
            pltpu.SemaphoreType.DMA((10,)),
        ],
        compiler_params=limits(32),
        cost_estimate=pl.CostEstimate(
            flops=2 * rows * channels * cells,
            bytes_accessed=4 * rows * channels,
            transcendentals=0,
        ),
    )(low, own, high, cot, after)


def conv_terms(weights, field, mirror, height, breadth, own, up, down):
    count = weights.shape[1] // 9
    places = (down, own, up) if mirror else (up, own, down)
    for a in range(3):
        part = lax.dot_general(
            weights[a],
            field[...],
            (((1,), (0,)), ((), ())),
            preferred_element_type=jnp.float32,
        )
        for q in range(height):
            total = None
            for c in range(3):
                column = None
                for b in range(3):
                    source = q + (1 - b if mirror else b - 1)
                    if 0 <= source < height:
                        at = (b * 3 + c) * count
                        term = part[at : at + count, source * breadth : (source + 1) * breadth]
                        column = term if column is None else column + term
                moved = shift_lanes(column, 1 - c if mirror else c - 1, breadth)
                total = moved if total is None else total + moved
            places[a][:, q * breadth : (q + 1) * breadth] = total


def plane_terms(fore, vol, back, cot, height, breadth):
    count = fore.shape[1] // 9
    cells = vol.shape[1]

    def body(fore_ref, vol_ref, back_ref, cot_ref, own, up, down, token):
        token[0] = 0
        halves = [pl.ds(0, count), pl.ds(count, count)]
        conv_terms(
            fore_ref, vol_ref, False, height, breadth, *(r.at[halves[0]] for r in (own, up, down))
        )
        conv_terms(
            back_ref, cot_ref, True, height, breadth, *(r.at[halves[1]] for r in (own, up, down))
        )

    shape = jax.ShapeDtypeStruct((2 * count, cells), jnp.float32)
    return pl.pallas_call(
        body,
        out_shape=(shape, shape, shape, TOKEN),
        in_specs=[VMEM] * 4,
        out_specs=(VMEM, VMEM, VMEM, SMEM),
        compiler_params=limits(12),
        cost_estimate=pl.CostEstimate(
            flops=4 * fore.size * cells,
            bytes_accessed=4 * fore.size + 24 * count * cells,
            transcendentals=0,
        ),
    )(fore, vol, back, cot)


def local(volume, kernel, cotangent):
    count, planes, height, breadth = volume.shape
    cells = height * breadth
    channels = kernel.shape[3]
    slabs = lax.axis_size("space")
    parts = lax.axis_size("chan")
    member = lax.axis_index("chan")
    factor = 1.0 / math.sqrt(slabs * planes * cells)
    along_y, near_z, block, far_z = groups_of(slabs)
    up = [(i, i + 1) for i in range(slabs - 1)]
    down = [(i + 1, i) for i in range(slabs - 1)]

    cot_copies = spread(cotangent.reshape(count, height, breadth), parts)
    cot_all = exchange(cot_copies, "chan").reshape(channels, cells)
    vol = volume.reshape(count, cells)
    vol_low = lax.ppermute(vol, "space", up)
    vol_high = lax.ppermute(vol, "space", down)
    fore, back, ready = own_weights(kernel.reshape(TAPS, channels, channels), count)
    fore = fore.reshape(3, 9 * count, channels)
    back = back.reshape(3, 9 * count, channels)

    terms = weight_terms(vol_low, vol, vol_high, cot_all, ready, factor, height, breadth)
    pieces = exchange(terms.reshape(len(along_y[0]), -1, channels), "space", along_y)
    vol_all = lax.all_gather(vol, "chan", axis=0, tiled=True)
    own, upper, lower, done = plane_terms(fore, vol_all, back, cot_all, height, breadth)
    pieces = sum_pieces(pieces, vol_all).reshape(len(near_z[0]), -1, channels)
    near = sum_pieces(exchange(pieces, "space", near_z), done)
    far = lax.all_gather(near, "space", axis=0, axis_index_groups=far_z)
    from_low = lax.ppermute(upper, "space", up)
    from_high = lax.ppermute(lower, "space", down)
    packed = scaled(far, from_low, from_high).astype(jnp.float16)
    copies = jnp.broadcast_to(packed[None], (len(block[0]),) + packed.shape)
    whole = exchange(copies, "space", block).astype(jnp.float32)
    weight_grad = unscaled(whole, TAPS * count).reshape(3, 3, 3, count, channels)

    output, input_grad = finish(own, from_low, from_high, height, breadth, volume.dtype, far)
    return (output.reshape(volume.shape), input_grad.reshape(volume.shape), weight_grad)


def solution(mesh):
    return jax.shard_map(
        local,
        mesh=mesh,
        in_specs=(P("chan", "space", None, None), P(), P("chan", "space", None, None)),
        out_specs=(
            P("chan", "space", None, None),
            P("chan", "space", None, None),
            P(None, None, None, "chan", None),
        ),
        check_vma=False,
    )
```

```python
import math

import jax
import jax.numpy as jnp
from jax import lax
from jax.experimental import pallas as pl
from jax.experimental.pallas import tpu as pltpu
from jax.sharding import PartitionSpec as P

TAPS = 27
Y_CHIPS = 4
NEAR = 4


def groups_of(count):
    length = count // Y_CHIPS
    far = length // NEAR
    block = [
        [y * length + hop * NEAR + k for y in range(Y_CHIPS) for k in range(NEAR)]
        for hop in range(far)
    ]
    far_z = [
        [y * length + hop * NEAR + k for hop in range(far)]
        for y in range(Y_CHIPS)
        for k in range(NEAR)
    ]
    return block, far_z


def exchange(pieces, axis, groups=None):
    return lax.all_to_all(pieces, axis, 0, 0, tiled=True, axis_index_groups=groups)


VMEM = pl.BlockSpec(memory_space=pltpu.VMEM)
HBM = pl.BlockSpec(memory_space=pl.ANY)


def limits(mib=56):
    return pltpu.CompilerParams(vmem_limit_bytes=mib * 1024 * 1024)


TOKEN = jax.ShapeDtypeStruct((1,), jnp.int32)
SMEM = pl.BlockSpec(memory_space=pltpu.SMEM)


def own_weights(kernel, count):
    channels = kernel.shape[2]
    width = min(channels, 128)
    per = width // count

    def body(kernel_ref, fore, back, token, block, sems):
        token[0] = 0
        member = lax.axis_index("chan")
        lanes = pl.ds(pl.multiple_of((member // per) * width, width), width)
        rows = pl.ds(pl.multiple_of(member * count, count), count)
        moves = [
            pltpu.make_async_copy(kernel_ref.at[:, :, lanes], block, sems.at[0]),
            pltpu.make_async_copy(kernel_ref.at[:, rows, :], back, sems.at[1]),
        ]
        for move in moves:
            move.start()
        at = lax.broadcasted_iota(jnp.int32, (count, width), 1)
        row = lax.broadcasted_iota(jnp.int32, (count, width), 0)
        pick = jnp.where(at == row + (member % per) * count, 1.0, 0.0).astype(fore.dtype)
        moves[0].wait()
        for tap in range(TAPS):
            fore[tap] = lax.dot_general(
                pick, block[tap], (((1,), (1,)), ((), ())), preferred_element_type=jnp.float32
            ).astype(fore.dtype)
        moves[1].wait()

    shape = jax.ShapeDtypeStruct((TAPS, count, channels), kernel.dtype)
    return pl.pallas_call(
        body,
        out_shape=(shape, shape, TOKEN),
        in_specs=[HBM],
        out_specs=(VMEM, VMEM, SMEM),
        scratch_shapes=[
            pltpu.VMEM((TAPS, channels, width), kernel.dtype),
            pltpu.SemaphoreType.DMA((2,)),
        ],
        compiler_params=limits(),
    )(kernel)


def spread(block, copies):
    count, height, breadth = block.shape
    cells = height * breadth

    def body(block_ref, out, wide, flat, sems):
        wide[...] = block_ref[...].astype(jnp.float32)
        for q in range(height):
            flat[:, q * breadth : (q + 1) * breadth] = wide[:, q, :].astype(flat.dtype)
        moves = [pltpu.make_async_copy(flat, out.at[k], sems.at[k]) for k in range(copies)]
        for move in moves:
            move.start()
        for move in moves:
            move.wait()

    return pl.pallas_call(
        body,
        out_shape=jax.ShapeDtypeStruct((copies, count, cells), block.dtype),
        in_specs=[VMEM],
        out_specs=HBM,
        scratch_shapes=[
            pltpu.VMEM(block.shape, jnp.float32),
            pltpu.VMEM((count, cells), block.dtype),
            pltpu.SemaphoreType.DMA((copies,)),
        ],
        compiler_params=limits(),
    )(block)


def sum_pieces(pieces, after):
    count, rows, columns = pieces.shape

    def body(pieces_ref, after_ref, out):
        total = pieces_ref[0]
        for k in range(1, count):
            total = total + pieces_ref[k]
        out[...] = total

    return pl.pallas_call(
        body,
        out_shape=jax.ShapeDtypeStruct((rows, columns), pieces.dtype),
        in_specs=[VMEM, SMEM],
        out_specs=VMEM,
        compiler_params=limits(8),
        cost_estimate=pl.CostEstimate(
            flops=pieces.size, bytes_accessed=4 * pieces.size, transcendentals=0
        ),
    )(pieces, after)


TOP = 13.0
SPARE = 8


def scaled(pieces):
    count, rows, columns = pieces.shape

    def body(pieces_ref, out):
        value = pieces_ref[0]
        for k in range(1, count):
            value = value + pieces_ref[k]
        most = jnp.max(jnp.max(jnp.abs(value), axis=0, keepdims=True), axis=1, keepdims=True)
        power = jnp.floor(jnp.log2(jnp.maximum(most, 1e-34)))
        out[:rows, :] = value * jnp.exp2(TOP - power)
        out[rows:, :] = jnp.broadcast_to(power, (SPARE, columns))

    return pl.pallas_call(
        body,
        out_shape=jax.ShapeDtypeStruct((rows + SPARE, columns), pieces.dtype),
        in_specs=[VMEM],
        out_specs=VMEM,
        compiler_params=limits(32),
    )(pieces)


def unscaled(pieces, amount):
    count, height, columns = pieces.shape
    rows = height - SPARE
    spans = [(k * rows, min(rows, amount - k * rows)) for k in range(count) if k * rows < amount]

    def body(pieces_ref, out, held, sems):
        moves = []
        for k, (start, size) in enumerate(spans):
            power = pieces_ref[k, rows:, :][:1]
            held[start : start + size, :] = pieces_ref[k, :size, :] * jnp.exp2(power - TOP)
            span = pl.ds(start, size)
            moves.append(pltpu.make_async_copy(held.at[span], out.at[span], sems.at[k]))
            moves[-1].start()
        for move in moves:
            move.wait()

    return pl.pallas_call(
        body,
        out_shape=jax.ShapeDtypeStruct((amount, columns), pieces.dtype),
        in_specs=[VMEM],
        out_specs=HBM,
        scratch_shapes=[
            pltpu.VMEM((amount, columns), pieces.dtype),
            pltpu.SemaphoreType.DMA((len(spans),)),
        ],
        compiler_params=limits(32),
    )(pieces)


def finish(own, low, high, height, breadth, dtype, after):
    rows = own.shape[0]
    count = rows // 2

    def body(own_ref, low_ref, high_ref, after_ref, first, second, wide):
        for q in range(height):
            lanes = pl.ds(q * breadth, breadth)
            wide[:, q, :] = own_ref[:, lanes] + low_ref[:, lanes] + high_ref[:, lanes]
        first[...] = wide[:count].astype(dtype)
        second[...] = wide[count:].astype(dtype)

    shape = jax.ShapeDtypeStruct((count, height, breadth), dtype)
    return pl.pallas_call(
        body,
        out_shape=(shape, shape),
        in_specs=[VMEM] * 3 + [HBM],
        out_specs=(VMEM, VMEM),
        scratch_shapes=[pltpu.VMEM((rows, height, breadth), jnp.float32)],
        compiler_params=limits(8),
    )(own, low, high, after)


def shift_lanes(value, offset, lanes):
    if offset == 0:
        return value
    at = lax.broadcasted_iota(jnp.int32, value.shape, 1)
    if offset < 0:
        return jnp.where(at == 0, 0.0, pltpu.roll(value, 1, 1))
    return jnp.where(at == lanes - 1, 0.0, pltpu.roll(value, lanes - 1, 1))


def weight_terms(low, own, high, cot, after, factor, height, breadth):
    count, cells = own.shape
    channels = cot.shape[0]
    group = 3 * count
    rows = 9 * group + count

    def body(low_ref, own_ref, high_ref, cot_ref, after_ref, out, stack, held, out_sems):
        sent = []

        def send(start, size):
            move = pltpu.make_async_copy(
                held.at[pl.ds(start, size)], out.at[pl.ds(start, size)], out_sems.at[len(sent)]
            )
            move.start()
            sent.append(move)

        held[9 * group :, :] = jnp.zeros((count, channels), held.dtype)
        send(9 * group, count)
        edge = jnp.zeros((9 * count, breadth), stack.dtype)
        stack[:, :breadth] = edge
        stack[:, (height + 1) * breadth :] = edge
        for a, plane in enumerate((low_ref, own_ref, high_ref)):
            for q in range(height):
                row = plane[:, q * breadth : (q + 1) * breadth].astype(jnp.float32)
                for c in range(3):
                    at = (a * 3 + c) * count
                    stack[at : at + count, (q + 1) * breadth : (q + 2) * breadth] = shift_lanes(
                        row, c - 1, breadth
                    ).astype(stack.dtype)
        for b in range(3):
            part = lax.dot_general(
                stack[:, b * breadth : b * breadth + cells],
                cot_ref[...],
                (((1,), (1,)), ((), ())),
                preferred_element_type=jnp.float32,
            )
            for a in range(3):
                at = (a * 3 + b) * group
                held[at : at + group, :] = part[a * group : (a + 1) * group] * factor
                send(at, group)
        for move in sent:
            move.wait()

    return pl.pallas_call(
        body,
        out_shape=jax.ShapeDtypeStruct((rows, channels), jnp.float32),
        in_specs=[VMEM] * 4 + [SMEM],
        out_specs=HBM,
        scratch_shapes=[
            pltpu.VMEM((9 * count, cells + 2 * breadth), own.dtype),
            pltpu.VMEM((rows, channels), jnp.float32),
            pltpu.SemaphoreType.DMA((10,)),
        ],
        compiler_params=limits(32),
        cost_estimate=pl.CostEstimate(
            flops=2 * rows * channels * cells,
            bytes_accessed=4 * rows * channels,
            transcendentals=0,
        ),
    )(low, own, high, cot, after)


def conv_terms(weights, field, mirror, height, breadth, own, up, down):
    count = weights.shape[1] // 9
    places = (down, own, up) if mirror else (up, own, down)
    for a in range(3):
        part = lax.dot_general(
            weights[a],
            field[...],
            (((1,), (0,)), ((), ())),
            preferred_element_type=jnp.float32,
        )
        for q in range(height):
            total = None
            for c in range(3):
                column = None
                for b in range(3):
                    source = q + (1 - b if mirror else b - 1)
                    if 0 <= source < height:
                        at = (b * 3 + c) * count
                        term = part[at : at + count, source * breadth : (source + 1) * breadth]
                        column = term if column is None else column + term
                moved = shift_lanes(column, 1 - c if mirror else c - 1, breadth)
                total = moved if total is None else total + moved
            places[a][:, q * breadth : (q + 1) * breadth] = total


def plane_terms(fore, vol, back, cot, height, breadth):
    count = fore.shape[1] // 9
    cells = vol.shape[1]

    def body(fore_ref, vol_ref, back_ref, cot_ref, own, up, down, token):
        token[0] = 0
        halves = [pl.ds(0, count), pl.ds(count, count)]
        conv_terms(
            fore_ref, vol_ref, False, height, breadth, *(r.at[halves[0]] for r in (own, up, down))
        )
        conv_terms(
            back_ref, cot_ref, True, height, breadth, *(r.at[halves[1]] for r in (own, up, down))
        )

    shape = jax.ShapeDtypeStruct((2 * count, cells), jnp.float32)
    return pl.pallas_call(
        body,
        out_shape=(shape, shape, shape, TOKEN),
        in_specs=[VMEM] * 4,
        out_specs=(VMEM, VMEM, VMEM, SMEM),
        compiler_params=limits(12),
        cost_estimate=pl.CostEstimate(
            flops=4 * fore.size * cells,
            bytes_accessed=4 * fore.size + 24 * count * cells,
            transcendentals=0,
        ),
    )(fore, vol, back, cot)


def local(volume, kernel, cotangent):
    count, planes, height, breadth = volume.shape
    cells = height * breadth
    channels = kernel.shape[3]
    slabs = lax.axis_size("space")
    parts = lax.axis_size("chan")
    member = lax.axis_index("chan")
    factor = 1.0 / math.sqrt(slabs * planes * cells)
    block, far_z = groups_of(slabs)
    up = [(i, i + 1) for i in range(slabs - 1)]
    down = [(i + 1, i) for i in range(slabs - 1)]

    cot_copies = spread(cotangent.reshape(count, height, breadth), parts)
    cot_all = exchange(cot_copies, "chan").reshape(channels, cells)
    vol = volume.reshape(count, cells)
    vol_low = lax.ppermute(vol, "space", up)
    vol_high = lax.ppermute(vol, "space", down)
    fore, back, ready = own_weights(kernel.reshape(TAPS, channels, channels), count)
    fore = fore.reshape(3, 9 * count, channels)
    back = back.reshape(3, 9 * count, channels)

    terms = weight_terms(vol_low, vol, vol_high, cot_all, ready, factor, height, breadth)
    pieces = exchange(terms.reshape(len(block[0]), -1, channels), "space", block)
    vol_all = lax.all_gather(vol, "chan", axis=0, tiled=True)
    own, upper, lower, done = plane_terms(fore, vol_all, back, cot_all, height, breadth)
    near = sum_pieces(pieces, done)
    far = lax.all_gather(near, "space", axis=0, axis_index_groups=far_z)
    from_low = lax.ppermute(upper, "space", up)
    from_high = lax.ppermute(lower, "space", down)
    packed = scaled(far).astype(jnp.float16)
    copies = jnp.broadcast_to(packed[None], (len(block[0]),) + packed.shape)
    whole = exchange(copies, "space", block).astype(jnp.float32)
    weight_grad = unscaled(whole, TAPS * count).reshape(3, 3, 3, count, channels)

    output, input_grad = finish(own, from_low, from_high, height, breadth, volume.dtype, far)
    return (output.reshape(volume.shape), input_grad.reshape(volume.shape), weight_grad)


def solution(mesh):
    return jax.shard_map(
        local,
        mesh=mesh,
        in_specs=(P("chan", "space", None, None), P(), P("chan", "space", None, None)),
        out_specs=(
            P("chan", "space", None, None),
            P("chan", "space", None, None),
            P(None, None, None, "chan", None),
        ),
        check_vma=False,
    )
```
